512 devices in a mesh: fsdp: 32 (over z, x), mp: 16 (over y, core).
Axes of the slice: x: 4, y: 8, z: 8, core: 2. Of those that a mesh axis runs over, the one named last changes fastest.
Arguments:
- tokens: bfloat16 [12288, 2048], P('fsdp', 'mp'), may hold values from -6 to 6
- cotangent: bfloat16 [12288, 2048], P('fsdp', 'mp'), may hold values from -6 to 6
- gate_weight: bfloat16 [2048, 6144], P('fsdp', 'mp'), may hold values from -0.125 to 0.125
- up_weight: bfloat16 [2048, 6144], P('fsdp', 'mp'), may hold values from -0.125 to 0.125
- down_weight: bfloat16 [2048, 6144], P('fsdp', 'mp'), may hold values from -0.125 to 0.125
Outputs:
- input_grad: bfloat16 [12288, 2048], P('fsdp', 'mp')
- grad_down: bfloat16 [2048, 6144], P('fsdp', 'mp')
The draws below stay inside these ranges and needn't reach their ends.
All inputs are finite; a program needn't handle non-finite values.
Results may differ from the reference program's by a relative error of at most 0.022.
Values may be sent and summed in bfloat16 or wider, within the bound.
No kernel may reach another device: no remote copies, remote signals or barrier semaphores. Data moves between devices by JAX's collectives and lax.ppermute only.
A program may use at most 64 MiB of HBM per device.

```python
import math
import jax
import jax.numpy as jnp
from jax import lax

D = 2048
FF = 6144
TOK_DEV = 384
TOKENS = 12288
N_FSDP = 32
N_MP = 16


def with_spikes(values, key, source, target, shards_of, factor):
    owner, partner = [(jnp.arange(values.shape[dim]) // (values.shape[dim] // shards_of)).reshape([-1 if axis == dim else 1 for axis in range(values.ndim)]) for dim in (source, target)]
    chosen = jax.random.permutation(key, shards_of)[partner]
    strong = (owner == chosen) | (owner == (partner + shards_of // 2) % shards_of)
    return jnp.where(strong, factor * values, values)


def steps_of(own_key, dims, pieces, low, top_value):
    factor_of, own = 1.0, jax.random.fold_in(own_key, 6)
    for position, blocks in pieces:
        steps = jnp.exp(jax.random.uniform(jax.random.fold_in(own, position), (blocks,), jnp.float32, low / len(pieces), top_value / len(pieces)))
        factor_of = factor_of * jnp.repeat(steps, dims[position] // blocks).reshape([-1 if axis == position else 1 for axis in range(len(dims))])
    return factor_of


def gaussian(key, dims, spread, reach, split=(), kind=jnp.bfloat16):
    values = jax.random.normal(key, dims, jnp.float32) * spread
    if len(split) > 0:
        values = steps_of(key, dims, split, -0.22, 0.18) * values
    return jnp.clip(values, min=-reach, max=reach).astype(kind)


def bell_draw_with(stream_key, dims, spread, limit, pieces, heavy, held_as=jnp.bfloat16):
    values = spread * jax.random.normal(stream_key, dims, jnp.float32)
    if pieces:
        values = values * steps_of(stream_key, dims, pieces, -0.22, 0.18)
    return jnp.clip(with_spikes(values, jax.random.fold_in(stream_key, 3), *heavy), -limit, limit).astype(held_as)


def setup_inputs(seed: int = 0) -> dict:
    key_list = jax.random.split(jax.random.key(seed), 6)
    return {
        "tokens": gaussian(key_list[0], (TOKENS, D), 1.0, 6.0, ((0, 32), (1, 16))),
        "cotangent": bell_draw_with(key_list[1], (TOKENS, D), 1.0, 6.0, ((0, 32), (1, 16)), (0, 1, 32, 2.75)),
        "gate_weight": gaussian(key_list[2], (D, FF), D ** -0.5, 0.125, ((0, 32), (1, 16))),
        "up_weight": gaussian(key_list[3], (D, FF), D ** -0.5, 0.125, ((0, 32), (1, 16))),
        "down_weight": gaussian(key_list[4], (D, FF), D ** -0.5, 0.125, ((0, 32), (1, 16))),
    }


def contract_last(left, right):
    return lax.dot_general(left, right, (((1,), (1,)), ((), ())), preferred_element_type=jnp.float32)

def reference(tokens, cotangent, gate_weight, up_weight, down_weight):
    gate_value = jnp.dot(tokens, gate_weight, preferred_element_type=jnp.float32)
    up_value = jnp.dot(tokens, up_weight, preferred_element_type=jnp.float32)
    sigmoid_gate = jax.nn.sigmoid(gate_value)
    hidden = (gate_value * sigmoid_gate * up_value).astype(jnp.bfloat16)
    hidden_grad = jnp.dot(cotangent, down_weight, preferred_element_type=jnp.float32)
    gate_grad = (hidden_grad * up_value * sigmoid_gate * (1.0 + gate_value * (1.0 - sigmoid_gate))).astype(jnp.bfloat16)
    up_grad = (hidden_grad * gate_value * sigmoid_gate).astype(jnp.bfloat16)
    group_width = FF // N_MP

    def add_hidden_group(running, group_index):
        offset = (group_index * group_width).astype(jnp.int32)
        part_gate = lax.dynamic_slice_in_dim(gate_grad, offset, group_width, 1)
        part_up = lax.dynamic_slice_in_dim(up_grad, offset, group_width, 1)
        weight_gate = lax.dynamic_slice_in_dim(gate_weight, offset, group_width, 1)
        weight_up = lax.dynamic_slice_in_dim(up_weight, offset, group_width, 1)
        partial_value = contract_last(part_gate, weight_gate) + contract_last(part_up, weight_up)
        rounded = lax.optimization_barrier(partial_value.astype(jnp.bfloat16))
        return (running + rounded.astype(jnp.float32), None)
    input_total, _ = lax.scan(add_hidden_group, jnp.zeros((TOKENS, D), jnp.float32), jnp.arange(N_MP, dtype=jnp.int32))
    input_grad = input_total.astype(jnp.bfloat16)

    def add_group(running, group_index):
        offset = (group_index * TOK_DEV).astype(jnp.int32)
        group_cot = lax.dynamic_slice_in_dim(cotangent, offset, TOK_DEV, 0)
        group_hidden = lax.dynamic_slice_in_dim(hidden, offset, TOK_DEV, 0)
        partial_value = lax.dot_general(group_cot, group_hidden, (((0,), (0,)), ((), ())), preferred_element_type=jnp.float32)
        rounded = lax.optimization_barrier(partial_value.astype(jnp.bfloat16))
        return (running + rounded.astype(jnp.float32), None)
    running, _ = lax.scan(add_group, jnp.zeros((D, FF), jnp.float32), jnp.arange(N_FSDP, dtype=jnp.int32))
    grad_down = (running * (1.0 / math.sqrt(TOKENS))).astype(jnp.bfloat16)
    return (input_grad, grad_down)
```

```python
import math

import jax
import jax.numpy as jnp
from jax import lax
from jax.sharding import PartitionSpec as P

N_Z = 8
N_X = 4
Z_GROUPS = [[z * N_X + x for z in range(N_Z)] for x in range(N_X)]
X_GROUPS = [[z * N_X + x for x in range(N_X)] for z in range(N_Z)]


def dot(left, right, dims):
    return lax.dot_general(left, right, (dims, ((), ())), preferred_element_type=jnp.float32)


def gather_weights(gate_weight, up_weight, down_weight):
    stacked = jnp.stack([gate_weight, up_weight, down_weight])
    along_z = lax.all_gather(stacked, "fsdp", axis_index_groups=Z_GROUPS, axis=0)
    along_x = lax.all_gather(along_z, "fsdp", axis_index_groups=X_GROUPS, axis=0)
    ordered = along_x.transpose(2, 1, 0, 3, 4)
    return ordered.reshape(3, N_Z * N_X * gate_weight.shape[0], gate_weight.shape[1])


def gather_rows(tokens, cotangent):
    count = lax.axis_size("mp")
    mine = jnp.stack([tokens, cotangent])
    blocks = [mine] + [
        lax.ppermute(mine, "mp", [(i, (i - shift) % count) for i in range(count)])
        for shift in range(1, count)
    ]
    relative = jnp.stack(blocks)
    me = lax.axis_index("mp")
    ordered = jnp.roll(relative, me, axis=0)
    rows = ordered.transpose(1, 2, 0, 3).reshape(2, tokens.shape[0], count * tokens.shape[1])
    return rows[0], rows[1]


def on_device(tokens, cotangent, gate_weight, up_weight, down_weight):
    n_fsdp, n_mp = lax.axis_size("fsdp"), lax.axis_size("mp")
    factor = 1.0 / math.sqrt(tokens.shape[0] * n_fsdp)
    gate_full, up_full, down_full = gather_weights(gate_weight, up_weight, down_weight)
    token_rows, cotangent_rows = gather_rows(tokens, cotangent)

    gate_value = dot(token_rows, gate_full, ((1,), (0,)))
    up_value = dot(token_rows, up_full, ((1,), (0,)))
    sigmoid_gate = jax.nn.sigmoid(gate_value)
    hidden = (gate_value * sigmoid_gate * up_value).astype(jnp.bfloat16)

    down_partial = dot(cotangent_rows, hidden, ((0,), (0,))).astype(jnp.bfloat16)
    down_blocks = down_partial.reshape(n_fsdp, -1, down_partial.shape[1])
    down_blocks = lax.all_to_all(down_blocks, "fsdp", 0, 0)
    grad_down = (down_blocks.astype(jnp.float32).sum(0) * factor).astype(jnp.bfloat16)

    hidden_grad = dot(cotangent_rows, down_full, ((1,), (0,)))
    gate_grad = (
        hidden_grad * up_value * sigmoid_gate * (1.0 + gate_value * (1.0 - sigmoid_gate))
    ).astype(jnp.bfloat16)
    up_grad = (hidden_grad * gate_value * sigmoid_gate).astype(jnp.bfloat16)
    partial_value = (
        dot(gate_grad, gate_full, ((1,), (1,))) + dot(up_grad, up_full, ((1,), (1,)))
    ).astype(jnp.bfloat16)
    blocks = partial_value.reshape(partial_value.shape[0], n_mp, -1).transpose(1, 0, 2)
    blocks = lax.all_to_all(blocks, "mp", 0, 0)
    input_grad = blocks.astype(jnp.float32).sum(0).astype(jnp.bfloat16)
    return (input_grad, grad_down)


def solution(mesh):
    placed = P("fsdp", "mp")
    return jax.shard_map(
        on_device,
        mesh=mesh,
        in_specs=(placed,) * 5,
        out_specs=(placed, placed),
        check_vma=False,
    )
```

```python
import math

import jax
import jax.numpy as jnp
from jax import lax
from jax.sharding import PartitionSpec as P

N_Z = 8
N_X = 4
N_Y = 8
N_CORE = 2
Z_GROUPS = [[z * N_X + x for z in range(N_Z)] for x in range(N_X)]
Y_GROUPS = [[y * N_CORE + c for y in range(N_Y)] for c in range(N_CORE)]


def dot(left, right, dims):
    return lax.dot_general(left, right, (dims, ((), ())), preferred_element_type=jnp.float32)


def send_x(value, step):
    pairs = [
        (z * N_X + x, z * N_X + (x + step) % N_X) for z in range(N_Z) for x in range(N_X)
    ]
    return lax.ppermute(value, "fsdp", pairs)


def send_core(value):
    pairs = [(i, i ^ 1) for i in range(N_Y * N_CORE)]
    return lax.ppermute(value, "mp", pairs)


def gather_z(block):
    copies = jnp.broadcast_to(block[None], (N_Z,) + block.shape)
    return lax.all_to_all(copies, "fsdp", 0, 0, axis_index_groups=Z_GROUPS)


def gather_x(own, me):
    half = N_Z // 2
    from_left = send_x(own, 1)
    from_right = send_x(own, -1)
    far_low = send_x(from_left[:half], 1)
    far_high = send_x(from_right[half:], -1)
    full = jnp.zeros((N_Z, N_X) + own.shape[1:], own.dtype)
    left, right, far = (me + N_X - 1) % N_X, (me + 1) % N_X, (me + 2) % N_X
    put = lambda into, block, z, x: lax.dynamic_update_slice(into, block[:, None], (z, x, 0, 0))
    full = put(full, own, 0, me)
    full = put(full, from_left, 0, left)
    full = put(full, from_right, 0, right)
    full = put(full, far_low, 0, far)
    full = put(full, far_high, half, far)
    return full


def add(left, right):
    return left.astype(jnp.float32) + right.astype(jnp.float32)


def scatter_x(partial_value, me):
    half = N_Z // 2
    take = lambda x, lo, hi: lax.dynamic_index_in_dim(partial_value, x, 1, keepdims=False)[lo:hi]
    left, right, far = (me + N_X - 1) % N_X, (me + 1) % N_X, (me + 2) % N_X
    low = send_x(take(far, 0, half), 1)
    high = send_x(take(far, half, N_Z), -1)
    to_right = jnp.concatenate(
        [add(take(right, 0, half), low).astype(jnp.bfloat16), take(right, half, N_Z)]
    )
    to_left = jnp.concatenate(
        [take(left, 0, half), add(take(left, half, N_Z), high).astype(jnp.bfloat16)]
    )
    from_left = send_x(to_right, 1)
    from_right = send_x(to_left, -1)
    return add(take(me, 0, N_Z), from_left) + from_right.astype(jnp.float32)


def on_device(tokens, cotangent, gate_weight, up_weight, down_weight):
    n_fsdp = lax.axis_size("fsdp")
    rows, width = tokens.shape
    depth, cols = gate_weight.shape
    factor = 1.0 / math.sqrt(rows * n_fsdp)
    me_x = lax.axis_index("fsdp") % N_X
    core = lax.axis_index("mp") % N_CORE

    stacked = jnp.concatenate([tokens, cotangent])
    gathered = lax.all_gather(stacked, "mp", axis=1, tiled=True)
    token_rows, cotangent_rows = gathered[:rows], gathered[rows:]

    gate_up = gather_x(gather_z(jnp.concatenate([gate_weight, up_weight])), me_x)
    gate_full = gate_up[:, :, :depth].reshape(-1, cols)
    up_full = gate_up[:, :, depth:].reshape(-1, cols)
    down_full = gather_x(gather_z(down_weight), me_x).reshape(-1, cols)

    gate_value = dot(token_rows, gate_full, ((1,), (0,)))
    up_value = dot(token_rows, up_full, ((1,), (0,)))
    sigmoid_gate = jax.nn.sigmoid(gate_value)
    hidden = (gate_value * sigmoid_gate * up_value).astype(jnp.bfloat16)

    down_partial = dot(cotangent_rows, hidden, ((0,), (0,))).astype(jnp.bfloat16)
    down_x = scatter_x(down_partial.reshape(N_Z, N_X, depth, cols), me_x)
    down_z = lax.all_to_all(
        down_x.astype(jnp.bfloat16), "fsdp", 0, 0, axis_index_groups=Z_GROUPS
    )
    grad_down = (down_z.astype(jnp.float32).sum(0) * factor).astype(jnp.bfloat16)

    hidden_grad = dot(cotangent_rows, down_full, ((1,), (0,)))
    gate_grad = (
        hidden_grad * up_value * sigmoid_gate * (1.0 + gate_value * (1.0 - sigmoid_gate))
    ).astype(jnp.bfloat16)
    up_grad = (hidden_grad * gate_value * sigmoid_gate).astype(jnp.bfloat16)
    partial_value = (
        dot(gate_grad, gate_full, ((1,), (1,))) + dot(up_grad, up_full, ((1,), (1,)))
    ).astype(jnp.bfloat16)
    blocks = partial_value.reshape(rows, N_Y, N_CORE, width).transpose(2, 1, 0, 3)
    mine = lax.dynamic_index_in_dim(blocks, core, 0, keepdims=False)
    other = lax.dynamic_index_in_dim(blocks, 1 - core, 0, keepdims=False)
    pair_sum = add(mine, send_core(other)).astype(jnp.bfloat16)
    summed = lax.all_to_all(pair_sum, "mp", 0, 0, axis_index_groups=Y_GROUPS)
    input_grad = summed.astype(jnp.float32).sum(0).astype(jnp.bfloat16)
    return (input_grad, grad_down)


def solution(mesh):
    placed = P("fsdp", "mp")
    return jax.shard_map(
        on_device,
        mesh=mesh,
        in_specs=(placed,) * 5,
        out_specs=(placed, placed),
        check_vma=False,
    )
```

```python
import math

import jax
import jax.numpy as jnp
from jax import lax
from jax.sharding import PartitionSpec as P

N_Z = 8
N_X = 4
N_Y = 8
N_CORE = 2
Z_GROUPS = [[z * N_X + x for z in range(N_Z)] for x in range(N_X)]
Y_GROUPS = [[y * N_CORE + c for y in range(N_Y)] for c in range(N_CORE)]


def dot(left, right, dims):
    return lax.dot_general(left, right, (dims, ((), ())), preferred_element_type=jnp.float32)


def send_x(value, step):
    pairs = [
        (z * N_X + x, z * N_X + (x + step) % N_X) for z in range(N_Z) for x in range(N_X)
    ]
    return lax.ppermute(value, "fsdp", pairs)


def send_core(value):
    pairs = [(i, i ^ 1) for i in range(N_Y * N_CORE)]
    return lax.ppermute(value, "mp", pairs)


def gather_z(block):
    copies = jnp.broadcast_to(block[None], (N_Z,) + block.shape)
    return lax.all_to_all(copies, "fsdp", 0, 0, axis_index_groups=Z_GROUPS)


def around_x(own):
    half = own.shape[0] // 2
    from_left = send_x(own, 1)
    from_right = send_x(own, -1)
    far_low = send_x(from_left[:half], 1)
    far_high = send_x(from_right[half:], -1)
    return from_left, from_right, far_low, far_high


def add(left, right):
    return left.astype(jnp.float32) + right.astype(jnp.float32)


def neighbours(me):
    return (me + N_X - 1) % N_X, (me + 1) % N_X, (me + 2) % N_X


def put_x(blocks, me):
    own, from_left, from_right, far_low, far_high = blocks
    n_z, rows, cols = own.shape
    left, right, far = neighbours(me)
    full = jnp.zeros((N_CORE, n_z, N_X // N_CORE, rows, cols), own.dtype)
    for block, x, z in (
        (own, me, 0),
        (from_left, left, 0),
        (from_right, right, 0),
        (far_low, far, 0),
        (far_high, far, n_z // 2),
    ):
        full = lax.dynamic_update_slice(full, block[None, :, None], (x // 2, z, x % 2, 0, 0))
    return full


def scatter_x(partial_value, me):
    half = N_Z // 2
    _, n_z, _, rows, cols = partial_value.shape
    left, right, far = neighbours(me)

    def take(x, low, high):
        return lax.dynamic_slice(
            partial_value, (x // 2, low, x % 2, 0, 0), (1, high - low, 1, rows, cols)
        ).reshape(high - low, rows, cols)

    low = send_x(take(far, 0, half), 1)
    high = send_x(take(far, half, N_Z), -1)
    to_right = jnp.concatenate(
        [add(take(right, 0, half), low).astype(jnp.bfloat16), take(right, half, N_Z)]
    )
    to_left = jnp.concatenate(
        [take(left, 0, half), add(take(left, half, N_Z), high).astype(jnp.bfloat16)]
    )
    from_left = send_x(to_right, 1)
    from_right = send_x(to_left, -1)
    return add(take(me, 0, N_Z), from_left) + from_right.astype(jnp.float32)


def on_device(tokens, cotangent, gate_weight, up_weight, down_weight):
    n_fsdp = lax.axis_size("fsdp")
    rows, width = tokens.shape
    depth, cols = gate_weight.shape
    n_feat = depth * n_fsdp
    factor = 1.0 / math.sqrt(rows * n_fsdp)
    me_x = lax.axis_index("fsdp") % N_X
    core = lax.axis_index("mp") % N_CORE

    stacked = jnp.concatenate([tokens, cotangent])
    own_core = lax.all_gather(stacked, "mp", axis_index_groups=Y_GROUPS, axis=1, tiled=True)
    other_core = send_core(own_core)
    both = jnp.zeros((2 * rows, n_feat), tokens.dtype)
    both = lax.dynamic_update_slice(both, own_core, (0, core * N_Y * width))
    both = lax.dynamic_update_slice(both, other_core, (0, (1 - core) * N_Y * width))
    token_rows, cotangent_rows = both[:rows], both[rows:]

    gate_up = gather_z(jnp.concatenate([gate_weight, up_weight]))
    around = (gate_up,) + around_x(gate_up)
    gate_full = put_x([b[:, :depth] for b in around], me_x).reshape(-1, cols)
    up_full = put_x([b[:, depth:] for b in around], me_x).reshape(-1, cols)

    pieces = down_weight.reshape(4, depth // 4, cols)
    from_left, from_right, far_low, far_high = around_x(pieces)
    left, right, far = neighbours(me_x)
    far_block = jnp.concatenate([far_low, far_high])
    down_x = jnp.zeros((N_X, depth, cols), down_weight.dtype)
    for block, x in ((pieces, me_x), (from_left, left), (from_right, right), (far_block, far)):
        down_x = lax.dynamic_update_slice(down_x, block.reshape(1, depth, cols), (x, 0, 0))
    down_full = lax.all_gather(
        down_x.reshape(N_CORE, -1, cols), "fsdp", axis_index_groups=Z_GROUPS, axis=1, tiled=True
    ).reshape(-1, cols)

    gate_value = dot(token_rows, gate_full, ((1,), (0,)))
    up_value = dot(token_rows, up_full, ((1,), (0,)))
    sigmoid_gate = jax.nn.sigmoid(gate_value)
    hidden = (gate_value * sigmoid_gate * up_value).astype(jnp.bfloat16)

    down_partial = dot(cotangent_rows, hidden, ((0,), (0,))).astype(jnp.bfloat16)
    down_z = scatter_x(down_partial.reshape(N_CORE, N_Z, N_X // N_CORE, depth, cols), me_x)
    down_z = lax.all_to_all(
        down_z.astype(jnp.bfloat16), "fsdp", 0, 0, axis_index_groups=Z_GROUPS
    )
    grad_down = (down_z.astype(jnp.float32).sum(0) * factor).astype(jnp.bfloat16)

    hidden_grad = dot(cotangent_rows, down_full, ((1,), (0,)))
    gate_grad = (
        hidden_grad * up_value * sigmoid_gate * (1.0 + gate_value * (1.0 - sigmoid_gate))
    ).astype(jnp.bfloat16)
    up_grad = (hidden_grad * gate_value * sigmoid_gate).astype(jnp.bfloat16)

    def half_partial(which):
        gate_half = lax.dynamic_index_in_dim(gate_full.reshape(N_CORE, -1, cols), which, 0, False)
        up_half = lax.dynamic_index_in_dim(up_full.reshape(N_CORE, -1, cols), which, 0, False)
        value = dot(gate_grad, gate_half, ((1,), (1,))) + dot(up_grad, up_half, ((1,), (1,)))
        return value.astype(jnp.bfloat16).reshape(rows, N_Y, width).transpose(1, 0, 2)

    from_core = send_core(half_partial(1 - core))
    pair_sum = add(half_partial(core), from_core).astype(jnp.bfloat16)
    summed = lax.all_to_all(pair_sum, "mp", 0, 0, axis_index_groups=Y_GROUPS)
    input_grad = summed.astype(jnp.float32).sum(0).astype(jnp.bfloat16)
    return (input_grad, grad_down)


def solution(mesh):
    placed = P("fsdp", "mp")
    return jax.shard_map(
        on_device,
        mesh=mesh,
        in_specs=(placed,) * 5,
        out_specs=(placed, placed),
        check_vma=False,
    )
```

```python
import math

import jax
import jax.numpy as jnp
from jax import lax
from jax.sharding import PartitionSpec as P

N_Z = 8
N_X = 4
N_Y = 8
N_CORE = 2
Z_GROUPS = [[z * N_X + x for z in range(N_Z)] for x in range(N_X)]
Y_GROUPS = [[y * N_CORE + c for y in range(N_Y)] for c in range(N_CORE)]


def dot(left, right, dims):
    return lax.dot_general(left, right, (dims, ((), ())), preferred_element_type=jnp.float32)


def send_x(value, step):
    pairs = [
        (z * N_X + x, z * N_X + (x + step) % N_X) for z in range(N_Z) for x in range(N_X)
    ]
    return lax.ppermute(value, "fsdp", pairs)


def send_core(value):
    pairs = [(i, i ^ 1) for i in range(N_Y * N_CORE)]
    return lax.ppermute(value, "mp", pairs)


def gather_z(block):
    copies = jnp.broadcast_to(block[None], (N_Z,) + block.shape)
    return lax.all_to_all(copies, "fsdp", 0, 0, axis_index_groups=Z_GROUPS)


def around_x(own):
    half = own.shape[0] // 2
    from_left = send_x(own, 1)
    from_right = send_x(own, -1)
    far_low = send_x(from_left[:half], 1)
    far_high = send_x(from_right[half:], -1)
    return from_left, from_right, far_low, far_high


def add(left, right):
    return left.astype(jnp.float32) + right.astype(jnp.float32)


def neighbours(me):
    return (me + N_X - 1) % N_X, (me + 1) % N_X, (me + 2) % N_X


def put_x(blocks, me):
    own, from_left, from_right, far_low, far_high = blocks
    n_z, rows, cols = own.shape
    left, right, far = neighbours(me)
    full = jnp.zeros((n_z, N_X, rows, cols), own.dtype)
    for block, x, z in (
        (own, me, 0),
        (from_left, left, 0),
        (from_right, right, 0),
        (far_low, far, 0),
        (far_high, far, n_z // 2),
    ):
        full = lax.dynamic_update_slice(full, block[:, None], (z, x, 0, 0))
    return full


def scatter_x(partial_value, me):
    half = N_Z // 2
    left, right, far = neighbours(me)

    def take(x, low, high):
        return lax.dynamic_index_in_dim(partial_value, x, 1, keepdims=False)[low:high]

    low = send_x(take(far, 0, half), 1)
    high = send_x(take(far, half, N_Z), -1)
    to_right = jnp.concatenate(
        [add(take(right, 0, half), low).astype(jnp.bfloat16), take(right, half, N_Z)]
    )
    to_left = jnp.concatenate(
        [take(left, 0, half), add(take(left, half, N_Z), high).astype(jnp.bfloat16)]
    )
    from_left = send_x(to_right, 1)
    from_right = send_x(to_left, -1)
    return add(take(me, 0, N_Z), from_left) + from_right.astype(jnp.float32)


def scatter_z(blocks, me):
    total = lax.dynamic_index_in_dim(blocks, me, 0, keepdims=False).astype(jnp.float32)
    for step in range(1, N_Z):
        pairs = [
            (z * N_X + x, (z + step) % N_Z * N_X + x) for z in range(N_Z) for x in range(N_X)
        ]
        out = lax.dynamic_index_in_dim(blocks, (me + step) % N_Z, 0, keepdims=False)
        total = total + lax.ppermute(out, "fsdp", pairs).astype(jnp.float32)
    return total


def on_device(tokens, cotangent, gate_weight, up_weight, down_weight):
    n_fsdp = lax.axis_size("fsdp")
    rows, width = tokens.shape
    depth, cols = gate_weight.shape
    factor = 1.0 / math.sqrt(rows * n_fsdp)
    me_x = lax.axis_index("fsdp") % N_X
    me_z = lax.axis_index("fsdp") // N_X
    core = lax.axis_index("mp") % N_CORE

    stacked = jnp.concatenate([tokens, cotangent])
    both = lax.all_gather(stacked, "mp", axis=1, tiled=True)
    token_rows, cotangent_rows = both[:rows], both[rows:]

    gate_up = gather_z(jnp.concatenate([gate_weight, up_weight]))
    around = (gate_up,) + around_x(gate_up)
    gate_full = put_x([b[:, :depth] for b in around], me_x).reshape(-1, cols)
    up_full = put_x([b[:, depth:] for b in around], me_x).reshape(-1, cols)

    pieces = down_weight.reshape(4, depth // 4, cols)
    from_left, from_right, far_low, far_high = around_x(pieces)
    left, right, far = neighbours(me_x)
    far_block = jnp.concatenate([far_low, far_high])
    down_x = jnp.zeros((N_X, depth, cols), down_weight.dtype)
    for block, x in ((pieces, me_x), (from_left, left), (from_right, right), (far_block, far)):
        down_x = lax.dynamic_update_slice(down_x, block.reshape(1, depth, cols), (x, 0, 0))
    down_full = gather_z(down_x).reshape(-1, cols)

    gate_value = dot(token_rows, gate_full, ((1,), (0,)))
    up_value = dot(token_rows, up_full, ((1,), (0,)))
    sigmoid_gate = jax.nn.sigmoid(gate_value)
    hidden = (gate_value * sigmoid_gate * up_value).astype(jnp.bfloat16)

    down_partial = dot(cotangent_rows, hidden, ((0,), (0,))).astype(jnp.bfloat16)
    down_z = scatter_x(down_partial.reshape(N_Z, N_X, depth, cols), me_x)
    down_sum = scatter_z(down_z.astype(jnp.bfloat16), me_z)
    grad_down = (down_sum * factor).astype(jnp.bfloat16)

    hidden_grad = dot(cotangent_rows, down_full, ((1,), (0,)))
    gate_grad = (
        hidden_grad * up_value * sigmoid_gate * (1.0 + gate_value * (1.0 - sigmoid_gate))
    ).astype(jnp.bfloat16)
    up_grad = (hidden_grad * gate_value * sigmoid_gate).astype(jnp.bfloat16)

    def half_partial(which):
        pick = lambda full: lax.dynamic_index_in_dim(
            full.reshape(N_Y, N_CORE, width, cols), which, 1, keepdims=False
        ).reshape(N_Y * width, cols)
        value = dot(gate_grad, pick(gate_full), ((1,), (1,)))
        value = value + dot(up_grad, pick(up_full), ((1,), (1,)))
        return value.astype(jnp.bfloat16).reshape(rows, N_Y, width).transpose(1, 0, 2)

    from_core = send_core(half_partial(1 - core))
    pair_sum = add(half_partial(core), from_core).astype(jnp.bfloat16)
    summed = lax.all_to_all(pair_sum, "mp", 0, 0, axis_index_groups=Y_GROUPS)
    input_grad = summed.astype(jnp.float32).sum(0).astype(jnp.bfloat16)
    return (input_grad, grad_down)


def solution(mesh):
    placed = P("fsdp", "mp")
    return jax.shard_map(
        on_device,
        mesh=mesh,
        in_specs=(placed,) * 5,
        out_specs=(placed, placed),
        check_vma=False,
    )
```

```python
import math

import jax
import jax.numpy as jnp
from jax import lax
from jax.sharding import PartitionSpec as P

N_Z = 8
N_X = 4
N_Y = 8
N_CORE = 2
Z_GROUPS = [[z * N_X + x for z in range(N_Z)] for x in range(N_X)]
Y_GROUPS = [[y * N_CORE + c for y in range(N_Y)] for c in range(N_CORE)]


def dot(left, right, dims):
    return lax.dot_general(left, right, (dims, ((), ())), preferred_element_type=jnp.float32)


def send_x(value, step):
    pairs = [
        (z * N_X + x, z * N_X + (x + step) % N_X) for z in range(N_Z) for x in range(N_X)
    ]
    return lax.ppermute(value, "fsdp", pairs)


def send_core(value):
    pairs = [(i, i ^ 1) for i in range(N_Y * N_CORE)]
    return lax.ppermute(value, "mp", pairs)


def gather_z(block):
    copies = jnp.broadcast_to(block[None], (N_Z,) + block.shape)
    return lax.all_to_all(copies, "fsdp", 0, 0, axis_index_groups=Z_GROUPS)


def around_x(own):
    half = own.shape[0] // 2
    from_left = send_x(own, 1)
    from_right = send_x(own, -1)
    far_low = send_x(from_left[:half], 1)
    far_high = send_x(from_right[half:], -1)
    return from_left, from_right, far_low, far_high


def add(left, right):
    return left.astype(jnp.float32) + right.astype(jnp.float32)


def neighbours(me):
    return (me + N_X - 1) % N_X, (me + 1) % N_X, (me + 2) % N_X


def put_x(blocks, me):
    own, from_left, from_right, far_low, far_high = blocks
    n_z, rows, cols = own.shape
    left, right, far = neighbours(me)
    full = jnp.zeros((n_z, N_X, rows, cols), own.dtype)
    for block, x, z in (
        (own, me, 0),
        (from_left, left, 0),
        (from_right, right, 0),
        (far_low, far, 0),
        (far_high, far, n_z // 2),
    ):
        full = lax.dynamic_update_slice(full, block[:, None], (z, x, 0, 0))
    return full


def scatter_x(partial_value, me):
    half = N_Z // 2
    left, right, far = neighbours(me)

    def take(x, low, high):
        return lax.dynamic_index_in_dim(partial_value, x, 1, keepdims=False)[low:high]

    low = send_x(take(far, 0, half), 1)
    high = send_x(take(far, half, N_Z), -1)
    to_right = jnp.concatenate(
        [add(take(right, 0, half), low).astype(jnp.bfloat16), take(right, half, N_Z)]
    )
    to_left = jnp.concatenate(
        [take(left, 0, half), add(take(left, half, N_Z), high).astype(jnp.bfloat16)]
    )
    from_left = send_x(to_right, 1)
    from_right = send_x(to_left, -1)
    return add(take(me, 0, N_Z), from_left) + from_right.astype(jnp.float32)


def on_device(tokens, cotangent, gate_weight, up_weight, down_weight):
    n_fsdp = lax.axis_size("fsdp")
    rows, width = tokens.shape
    depth, cols = gate_weight.shape
    factor = 1.0 / math.sqrt(rows * n_fsdp)
    me_x = lax.axis_index("fsdp") % N_X
    core = lax.axis_index("mp") % N_CORE

    stacked = jnp.concatenate([tokens, cotangent])
    both = lax.all_gather(stacked, "mp", axis=1, tiled=True)
    token_rows, cotangent_rows = both[:rows], both[rows:]

    down_x = jnp.zeros((N_X, depth, cols), down_weight.dtype)
    down_x = lax.dynamic_update_slice(down_x, down_weight[None], (me_x, 0, 0))
    for step in (1, N_X - 1, 2):
        block = send_x(down_weight, step)
        down_x = lax.dynamic_update_slice(down_x, block[None], ((me_x - step) % N_X, 0, 0))

    gate_z = gather_z(gate_weight)
    gate_z, up_weight = lax.optimization_barrier((gate_z, up_weight))
    gate_full = put_x((gate_z,) + around_x(gate_z), me_x).reshape(-1, cols)
    up_z = gather_z(up_weight)
    up_z, down_x = lax.optimization_barrier((up_z, down_x))
    up_full = put_x((up_z,) + around_x(up_z), me_x).reshape(-1, cols)
    down_full = gather_z(down_x).reshape(-1, cols)

    gate_value = dot(token_rows, gate_full, ((1,), (0,)))
    up_value = dot(token_rows, up_full, ((1,), (0,)))
    sigmoid_gate = jax.nn.sigmoid(gate_value)
    hidden = (gate_value * sigmoid_gate * up_value).astype(jnp.bfloat16)

    hidden_grad = dot(cotangent_rows, down_full, ((1,), (0,)))
    gate_grad = (
        hidden_grad * up_value * sigmoid_gate * (1.0 + gate_value * (1.0 - sigmoid_gate))
    ).astype(jnp.bfloat16)
    up_grad = (hidden_grad * gate_value * sigmoid_gate).astype(jnp.bfloat16)

    def half_partial(which):
        pick = lambda full: lax.dynamic_index_in_dim(
            full.reshape(N_Y, N_CORE, width, cols), which, 1, keepdims=False
        ).reshape(N_Y * width, cols)
        value = dot(gate_grad, pick(gate_full), ((1,), (1,)))
        value = value + dot(up_grad, pick(up_full), ((1,), (1,)))
        return value.astype(jnp.bfloat16).reshape(rows, N_Y, width).transpose(1, 0, 2)

    from_core = send_core(half_partial(1 - core))
    pair_sum = add(half_partial(core), from_core).astype(jnp.bfloat16)
    pair_sum, hidden = lax.optimization_barrier((pair_sum, hidden))
    summed = lax.all_to_all(pair_sum, "mp", 0, 0, axis_index_groups=Y_GROUPS)

    down_partial = dot(cotangent_rows, hidden, ((0,), (0,))).astype(jnp.bfloat16)
    down_z = scatter_x(down_partial.reshape(N_Z, N_X, depth, cols), me_x).astype(jnp.bfloat16)
    summed, down_z = lax.optimization_barrier((summed, down_z))
    input_grad = summed.astype(jnp.float32).sum(0).astype(jnp.bfloat16)
    down_z = lax.all_to_all(down_z, "fsdp", 0, 0, axis_index_groups=Z_GROUPS)
    grad_down = (down_z.astype(jnp.float32).sum(0) * factor).astype(jnp.bfloat16)
    return (input_grad, grad_down)


def solution(mesh):
    placed = P("fsdp", "mp")
    return jax.shard_map(
        on_device,
        mesh=mesh,
        in_specs=(placed,) * 5,
        out_specs=(placed, placed),
        check_vma=False,
    )
```

```python
import math

import jax
import jax.numpy as jnp
from jax import lax
from jax.sharding import PartitionSpec as P

N_Z = 8
N_X = 4
N_Y = 8
N_CORE = 2
Z_GROUPS = [[z * N_X + x for z in range(N_Z)] for x in range(N_X)]
X_GROUPS = [[z * N_X + x for x in range(N_X)] for z in range(N_Z)]
Y_GROUPS = [[y * N_CORE + c for y in range(N_Y)] for c in range(N_CORE)]


def dot(left, right, dims):
    return lax.dot_general(left, right, (dims, ((), ())), preferred_element_type=jnp.float32)


def send_x(value, step):
    pairs = [
        (z * N_X + x, z * N_X + (x + step) % N_X) for z in range(N_Z) for x in range(N_X)
    ]
    return lax.ppermute(value, "fsdp", pairs)


def send_core(value):
    pairs = [(i, i ^ 1) for i in range(N_Y * N_CORE)]
    return lax.ppermute(value, "mp", pairs)


def gather_z(block):
    copies = jnp.broadcast_to(block[None], (N_Z,) + block.shape)
    return lax.all_to_all(copies, "fsdp", 0, 0, axis_index_groups=Z_GROUPS)


def add(left, right):
    return left.astype(jnp.float32) + right.astype(jnp.float32)


def put_x(blocks, me):
    n_z, rows, cols = blocks[0].shape
    full = jnp.zeros((n_z, N_X, rows, cols), blocks[0].dtype)
    for block, step in zip(blocks, (0, N_X - 1, 1, 2)):
        full = lax.dynamic_update_slice(full, block[:, None], (0, (me + step) % N_X, 0, 0))
    return full


def on_device(tokens, cotangent, gate_weight, up_weight, down_weight):
    n_fsdp = lax.axis_size("fsdp")
    rows, width = tokens.shape
    depth, cols = gate_weight.shape
    factor = 1.0 / math.sqrt(rows * n_fsdp)
    me_x = lax.axis_index("fsdp") % N_X
    core = lax.axis_index("mp") % N_CORE

    stacked = jnp.concatenate([tokens, cotangent])
    both = lax.all_gather(stacked, "mp", axis=1, tiled=True)
    token_rows, cotangent_rows = both[:rows], both[rows:]

    down_x = jnp.zeros((N_X, depth, cols), down_weight.dtype)
    down_x = lax.dynamic_update_slice(down_x, down_weight[None], (me_x, 0, 0))
    for step in (1, N_X - 1, 2):
        block = send_x(down_weight, step)
        down_x = lax.dynamic_update_slice(down_x, block[None], ((me_x - step) % N_X, 0, 0))

    gate_z = gather_z(gate_weight)
    gate_z, up_weight = lax.optimization_barrier((gate_z, up_weight))
    up_z = gather_z(up_weight)
    up_z, down_x = lax.optimization_barrier((up_z, down_x))
    down_full = gather_z(down_x).reshape(-1, cols)

    gate_left, gate_right = send_x(gate_z, 1), send_x(gate_z, -1)
    up_right, up_left = send_x(up_z, -1), send_x(up_z, 1)
    gate_far, up_far = send_x(gate_left, 1), send_x(up_right, -1)
    gate_full = put_x((gate_z, gate_left, gate_right, gate_far), me_x).reshape(-1, cols)
    up_full = put_x((up_z, up_left, up_right, up_far), me_x).reshape(-1, cols)

    gate_value = dot(token_rows, gate_full, ((1,), (0,)))
    up_value = dot(token_rows, up_full, ((1,), (0,)))
    sigmoid_gate = jax.nn.sigmoid(gate_value)
    hidden = (gate_value * sigmoid_gate * up_value).astype(jnp.bfloat16)

    down_partial = dot(cotangent_rows, hidden, ((0,), (0,))).astype(jnp.bfloat16)
    down_partial, cotangent_rows = lax.optimization_barrier((down_partial, cotangent_rows))
    hidden_grad = dot(cotangent_rows, down_full, ((1,), (0,)))
    gate_grad = (
        hidden_grad * up_value * sigmoid_gate * (1.0 + gate_value * (1.0 - sigmoid_gate))
    ).astype(jnp.bfloat16)
    up_grad = (hidden_grad * gate_value * sigmoid_gate).astype(jnp.bfloat16)

    def half_partial(which):
        pick = lambda full: lax.dynamic_index_in_dim(
            full.reshape(N_Y, N_CORE, width, cols), which, 1, keepdims=False
        ).reshape(N_Y * width, cols)
        value = dot(gate_grad, pick(gate_full), ((1,), (1,)))
        value = value + dot(up_grad, pick(up_full), ((1,), (1,)))
        return value.astype(jnp.bfloat16).reshape(rows, N_Y, width).transpose(1, 0, 2)

    from_core = send_core(half_partial(1 - core))
    pair_sum = add(half_partial(core), from_core).astype(jnp.bfloat16)
    summed = lax.all_to_all(pair_sum, "mp", 0, 0, axis_index_groups=Y_GROUPS)

    down_z = lax.psum_scatter(
        down_partial.reshape(N_Z, N_X, depth, cols).transpose(1, 0, 2, 3).reshape(-1, cols),
        "fsdp",
        scatter_dimension=0,
        axis_index_groups=X_GROUPS,
        tiled=True,
    ).reshape(N_Z, depth, cols)
    summed, down_z = lax.optimization_barrier((summed, down_z))
    input_grad = summed.astype(jnp.float32).sum(0).astype(jnp.bfloat16)
    down_z = lax.all_to_all(down_z, "fsdp", 0, 0, axis_index_groups=Z_GROUPS)
    grad_down = (down_z.astype(jnp.float32).sum(0) * factor).astype(jnp.bfloat16)
    return (input_grad, grad_down)


def solution(mesh):
    placed = P("fsdp", "mp")
    return jax.shard_map(
        on_device,
        mesh=mesh,
        in_specs=(placed,) * 5,
        out_specs=(placed, placed),
        check_vma=False,
    )
```

```python
import math

import jax
import jax.numpy as jnp
from jax import lax
from jax.sharding import PartitionSpec as P

N_Z = 8
N_X = 4
N_Y = 8
N_CORE = 2
Z_GROUPS = [[z * N_X + x for z in range(N_Z)] for x in range(N_X)]
X_GROUPS = [[z * N_X + x for x in range(N_X)] for z in range(N_Z)]
Y_GROUPS = [[y * N_CORE + c for y in range(N_Y)] for c in range(N_CORE)]


def dot(left, right, dims):
    return lax.dot_general(left, right, (dims, ((), ())), preferred_element_type=jnp.float32)


def send_x(value, step):
    pairs = [
        (z * N_X + x, z * N_X + (x + step) % N_X) for z in range(N_Z) for x in range(N_X)
    ]
    return lax.ppermute(value, "fsdp", pairs)


def send_core(value):
    pairs = [(i, i ^ 1) for i in range(N_Y * N_CORE)]
    return lax.ppermute(value, "mp", pairs)


def gather_z(block):
    copies = jnp.broadcast_to(block[None], (N_Z,) + block.shape)
    return lax.all_to_all(copies, "fsdp", 0, 0, axis_index_groups=Z_GROUPS)


def add(left, right):
    return left.astype(jnp.float32) + right.astype(jnp.float32)


def put_x(full, blocks, me, row):
    for block, step in zip(blocks, (0, N_X - 1, 1, 2)):
        full = lax.dynamic_update_slice(full, block[:, None], (0, (me + step) % N_X, row, 0))
    return full


def on_device(tokens, cotangent, gate_weight, up_weight, down_weight):
    n_fsdp = lax.axis_size("fsdp")
    rows, width = tokens.shape
    depth, cols = gate_weight.shape
    factor = 1.0 / math.sqrt(rows * n_fsdp)
    me_x = lax.axis_index("fsdp") % N_X
    core = lax.axis_index("mp") % N_CORE

    stacked = jnp.concatenate([tokens, cotangent])
    both = lax.all_gather(stacked, "mp", axis=1, tiled=True)
    token_rows, cotangent_rows = both[:rows], both[rows:]

    part = depth // 4
    piece_a = jnp.concatenate([gate_weight, down_weight[:part]])
    piece_b = jnp.concatenate([up_weight, down_weight[part : 2 * part]])
    rest = down_weight[2 * part :]
    rest_x = jnp.zeros((N_X,) + rest.shape, rest.dtype)
    rest_x = lax.dynamic_update_slice(rest_x, rest[None], (me_x, 0, 0))
    for step in (1, N_X - 1, 2):
        block = send_x(rest, step)
        rest_x = lax.dynamic_update_slice(rest_x, block[None], ((me_x - step) % N_X, 0, 0))

    a_own = gather_z(piece_a)
    a_own, piece_b = lax.optimization_barrier((a_own, piece_b))
    b_own = gather_z(piece_b)
    a_left, a_right = send_x(a_own, 1), send_x(a_own, -1)
    a_left, b_own = lax.optimization_barrier((a_left, b_own))
    b_right, b_left = send_x(b_own, -1), send_x(b_own, 1)
    b_right, rest_x = lax.optimization_barrier((b_right, rest_x))
    a_far, b_far = send_x(a_left, 1), send_x(b_right, -1)
    rest_z = gather_z(rest_x)

    a_blocks, b_blocks = (a_own, a_left, a_right, a_far), (b_own, b_left, b_right, b_far)
    empty = jnp.zeros((N_Z, N_X, depth, cols), gate_weight.dtype)
    gate_full = put_x(empty, [v[:, :depth] for v in a_blocks], me_x, 0).reshape(-1, cols)
    up_full = put_x(empty, [v[:, :depth] for v in b_blocks], me_x, 0).reshape(-1, cols)
    down_full = put_x(empty, [v[:, depth:] for v in a_blocks], me_x, 0)
    down_full = put_x(down_full, [v[:, depth:] for v in b_blocks], me_x, part)
    down_full = lax.dynamic_update_slice(down_full, rest_z, (0, 0, 2 * part, 0))
    down_full = down_full.reshape(-1, cols)

    gate_value = dot(token_rows, gate_full, ((1,), (0,)))
    up_value = dot(token_rows, up_full, ((1,), (0,)))
    sigmoid_gate = jax.nn.sigmoid(gate_value)
    hidden = (gate_value * sigmoid_gate * up_value).astype(jnp.bfloat16)

    down_partial = dot(cotangent_rows, hidden, ((0,), (0,))).astype(jnp.bfloat16)
    down_partial, cotangent_rows = lax.optimization_barrier((down_partial, cotangent_rows))
    hidden_grad = dot(cotangent_rows, down_full, ((1,), (0,)))
    gate_grad = (
        hidden_grad * up_value * sigmoid_gate * (1.0 + gate_value * (1.0 - sigmoid_gate))
    ).astype(jnp.bfloat16)
    up_grad = (hidden_grad * gate_value * sigmoid_gate).astype(jnp.bfloat16)

    def half_partial(which):
        pick = lambda full: lax.dynamic_index_in_dim(
            full.reshape(N_Y, N_CORE, width, cols), which, 1, keepdims=False
        ).reshape(N_Y * width, cols)
        value = dot(gate_grad, pick(gate_full), ((1,), (1,)))
        value = value + dot(up_grad, pick(up_full), ((1,), (1,)))
        return value.astype(jnp.bfloat16).reshape(rows, N_Y, width).transpose(1, 0, 2)

    from_core = send_core(half_partial(1 - core))
    pair_sum = add(half_partial(core), from_core).astype(jnp.bfloat16)
    summed = lax.all_to_all(pair_sum, "mp", 0, 0, axis_index_groups=Y_GROUPS)

    down_z = lax.psum_scatter(
        down_partial, "fsdp", scatter_dimension=0, axis_index_groups=Z_GROUPS, tiled=True
    ).reshape(N_X, depth, cols)
    summed, down_z = lax.optimization_barrier((summed, down_z))
    input_grad = summed.astype(jnp.float32).sum(0).astype(jnp.bfloat16)
    down_x = lax.all_to_all(down_z, "fsdp", 0, 0, axis_index_groups=X_GROUPS)
    grad_down = (down_x.astype(jnp.float32).sum(0) * factor).astype(jnp.bfloat16)
    return (input_grad, grad_down)


def solution(mesh):
    placed = P("fsdp", "mp")
    return jax.shard_map(
        on_device,
        mesh=mesh,
        in_specs=(placed,) * 5,
        out_specs=(placed, placed),
        check_vma=False,
    )
```

```python
import math

import jax
import jax.numpy as jnp
from jax import lax
from jax.sharding import PartitionSpec as P

N_Z = 8
N_X = 4
N_Y = 8
N_CORE = 2
Z_GROUPS = [[z * N_X + x for z in range(N_Z)] for x in range(N_X)]
X_GROUPS = [[z * N_X + x for x in range(N_X)] for z in range(N_Z)]
Y_GROUPS = [[y * N_CORE + c for y in range(N_Y)] for c in range(N_CORE)]


def dot(left, right, dims):
    return lax.dot_general(left, right, (dims, ((), ())), preferred_element_type=jnp.float32)


def send_x(value, step):
    pairs = [
        (z * N_X + x, z * N_X + (x + step) % N_X) for z in range(N_Z) for x in range(N_X)
    ]
    return lax.ppermute(value, "fsdp", pairs)


def send_core(value):
    pairs = [(i, i ^ 1) for i in range(N_Y * N_CORE)]
    return lax.ppermute(value, "mp", pairs)


def copies_of(block):
    return jnp.broadcast_to(block[None], (N_Z,) + block.shape)


def gather_z(copies):
    return lax.all_to_all(copies, "fsdp", 0, 0, axis_index_groups=Z_GROUPS)


def add(left, right):
    return left.astype(jnp.float32) + right.astype(jnp.float32)


def put_x(blocks, me):
    n_z, rows, cols = blocks[0].shape
    full = jnp.zeros((n_z, N_X, rows, cols), blocks[0].dtype)
    for block, step in zip(blocks, (0, N_X - 1, 1, 2)):
        full = lax.dynamic_update_slice(full, block[:, None], (0, (me + step) % N_X, 0, 0))
    return full


def on_device(tokens, cotangent, gate_weight, up_weight, down_weight):
    n_fsdp = lax.axis_size("fsdp")
    rows, width = tokens.shape
    depth, cols = gate_weight.shape
    factor = 1.0 / math.sqrt(rows * n_fsdp)
    me_x = lax.axis_index("fsdp") % N_X
    core = lax.axis_index("mp") % N_CORE

    gate_copies = copies_of(gate_weight)
    gate_copies, tokens, cotangent = lax.optimization_barrier((gate_copies, tokens, cotangent))
    stacked = jnp.concatenate([tokens, cotangent])
    both = lax.all_gather(stacked, "mp", axis=1, tiled=True)
    token_rows, cotangent_rows = both[:rows], both[rows:]

    down_x = jnp.zeros((N_X, depth, cols), down_weight.dtype)
    down_x = lax.dynamic_update_slice(down_x, down_weight[None], (me_x, 0, 0))
    for step in (1, N_X - 1, 2):
        block = send_x(down_weight, step)
        down_x = lax.dynamic_update_slice(down_x, block[None], ((me_x - step) % N_X, 0, 0))

    gate_z = gather_z(gate_copies)
    gate_left, gate_right = send_x(gate_z, 1), send_x(gate_z, -1)
    gate_z, up_copies = lax.optimization_barrier((gate_z, copies_of(up_weight)))
    up_z = gather_z(up_copies)
    up_z, down_copies, gate_left = lax.optimization_barrier((up_z, copies_of(down_x), gate_left))
    down_full = gather_z(down_copies).reshape(-1, cols)

    up_right, up_left = send_x(up_z, -1), send_x(up_z, 1)
    gate_far, up_far = send_x(gate_left, 1), send_x(up_right, -1)
    gate_full = put_x((gate_z, gate_left, gate_right, gate_far), me_x).reshape(-1, cols)
    up_full = put_x((up_z, up_left, up_right, up_far), me_x).reshape(-1, cols)

    gate_value = dot(token_rows, gate_full, ((1,), (0,)))
    up_value = dot(token_rows, up_full, ((1,), (0,)))
    sigmoid_gate = jax.nn.sigmoid(gate_value)
    hidden = (gate_value * sigmoid_gate * up_value).astype(jnp.bfloat16)

    down_partial = dot(cotangent_rows, hidden, ((0,), (0,))).astype(jnp.bfloat16)
    down_partial, cotangent_rows = lax.optimization_barrier((down_partial, cotangent_rows))
    hidden_grad = dot(cotangent_rows, down_full, ((1,), (0,)))
    gate_grad = (
        hidden_grad * up_value * sigmoid_gate * (1.0 + gate_value * (1.0 - sigmoid_gate))
    ).astype(jnp.bfloat16)
    up_grad = (hidden_grad * gate_value * sigmoid_gate).astype(jnp.bfloat16)

    def half_partial(which):
        pick = lambda full: lax.dynamic_index_in_dim(
            full.reshape(N_Y, N_CORE, width, cols), which, 1, keepdims=False
        ).reshape(N_Y * width, cols)
        value = dot(gate_grad, pick(gate_full), ((1,), (1,)))
        value = value + dot(up_grad, pick(up_full), ((1,), (1,)))
        return value.astype(jnp.bfloat16).reshape(rows, N_Y, width).transpose(1, 0, 2)

    from_core = send_core(half_partial(1 - core))
    pair_sum = add(half_partial(core), from_core).astype(jnp.bfloat16)
    summed = lax.all_to_all(pair_sum, "mp", 0, 0, axis_index_groups=Y_GROUPS)

    down_z = lax.psum_scatter(
        down_partial, "fsdp", scatter_dimension=0, axis_index_groups=Z_GROUPS, tiled=True
    ).reshape(N_X, depth, cols)
    down_sum = lax.dynamic_index_in_dim(down_z, me_x, 0, False).astype(jnp.float32)
    for step in (1, N_X - 1, 2):
        block = lax.dynamic_index_in_dim(down_z, (me_x + step) % N_X, 0, False)
        down_sum = down_sum + send_x(block, step).astype(jnp.float32)
    grad_down = (down_sum * factor).astype(jnp.bfloat16)
    input_grad = summed.astype(jnp.float32).sum(0).astype(jnp.bfloat16)
    return (input_grad, grad_down)


def solution(mesh):
    placed = P("fsdp", "mp")
    return jax.shard_map(
        on_device,
        mesh=mesh,
        in_specs=(placed,) * 5,
        out_specs=(placed, placed),
        check_vma=False,
    )
```

```python
import math

import jax
import jax.numpy as jnp
from jax import lax
from jax.sharding import PartitionSpec as P

N_Z = 8
N_X = 4
N_Y = 8
N_CORE = 2
Z_GROUPS = [[z * N_X + x for z in range(N_Z)] for x in range(N_X)]
X_GROUPS = [[z * N_X + x for x in range(N_X)] for z in range(N_Z)]
Y_GROUPS = [[y * N_CORE + c for y in range(N_Y)] for c in range(N_CORE)]


def dot(left, right, dims):
    return lax.dot_general(left, right, (dims, ((), ())), preferred_element_type=jnp.float32)


def send_x(value, step):
    pairs = [
        (z * N_X + x, z * N_X + (x + step) % N_X) for z in range(N_Z) for x in range(N_X)
    ]
    return lax.ppermute(value, "fsdp", pairs)


def send_core(value):
    pairs = [(i, i ^ 1) for i in range(N_Y * N_CORE)]
    return lax.ppermute(value, "mp", pairs)


def copies_of(block):
    return jnp.broadcast_to(block[None], (N_Z,) + block.shape)


def gather_z(copies):
    return lax.all_to_all(copies, "fsdp", 0, 0, axis_index_groups=Z_GROUPS)


def add(left, right):
    return left.astype(jnp.float32) + right.astype(jnp.float32)


def put_x(blocks, me):
    n_z, rows, cols = blocks[0].shape
    full = jnp.zeros((n_z, N_X, rows, cols), blocks[0].dtype)
    for block, step in zip(blocks, (0, N_X - 1, 1, 2)):
        full = lax.dynamic_update_slice(full, block[:, None], (0, (me + step) % N_X, 0, 0))
    return full


def on_device(tokens, cotangent, gate_weight, up_weight, down_weight):
    n_fsdp = lax.axis_size("fsdp")
    rows, width = tokens.shape
    depth, cols = gate_weight.shape
    factor = 1.0 / math.sqrt(rows * n_fsdp)
    me_x = lax.axis_index("fsdp") % N_X
    core = lax.axis_index("mp") % N_CORE

    gate_copies = copies_of(gate_weight)
    gate_copies, tokens, cotangent = lax.optimization_barrier((gate_copies, tokens, cotangent))
    stacked = jnp.concatenate([tokens, cotangent])
    both = lax.all_gather(stacked, "mp", axis=1, tiled=True)
    token_rows, cotangent_rows = both[:rows], both[rows:]

    gate_z = gather_z(gate_copies)
    gate_left, gate_right = send_x(gate_z, 1), send_x(gate_z, -1)
    gate_z, up_copies = lax.optimization_barrier((gate_z, copies_of(up_weight)))
    up_z = gather_z(up_copies)
    up_z, down_copies, gate_left = lax.optimization_barrier(
        (up_z, copies_of(down_weight), gate_left)
    )
    down_own = gather_z(down_copies)
    up_right, up_left = send_x(up_z, -1), send_x(up_z, 1)
    gate_far, up_far = send_x(gate_left, 1), send_x(up_right, -1)
    down_left, down_right = send_x(down_own, 1), send_x(down_own, -1)
    down_far = send_x(down_left, 1)
    gate_full = put_x((gate_z, gate_left, gate_right, gate_far), me_x).reshape(-1, cols)
    up_full = put_x((up_z, up_left, up_right, up_far), me_x).reshape(-1, cols)
    down_full = put_x((down_own, down_left, down_right, down_far), me_x).reshape(-1, cols)

    gate_value = dot(token_rows, gate_full, ((1,), (0,)))
    up_value = dot(token_rows, up_full, ((1,), (0,)))
    sigmoid_gate = jax.nn.sigmoid(gate_value)
    hidden = (gate_value * sigmoid_gate * up_value).astype(jnp.bfloat16)

    down_partial = dot(cotangent_rows, hidden, ((0,), (0,))).astype(jnp.bfloat16)
    down_partial, cotangent_rows = lax.optimization_barrier((down_partial, cotangent_rows))
    hidden_grad = dot(cotangent_rows, down_full, ((1,), (0,)))
    gate_grad = (
        hidden_grad * up_value * sigmoid_gate * (1.0 + gate_value * (1.0 - sigmoid_gate))
    ).astype(jnp.bfloat16)
    up_grad = (hidden_grad * gate_value * sigmoid_gate).astype(jnp.bfloat16)

    def half_partial(which):
        pick = lambda full: lax.dynamic_index_in_dim(
            full.reshape(N_Y, N_CORE, width, cols), which, 1, keepdims=False
        ).reshape(N_Y * width, cols)
        value = dot(gate_grad, pick(gate_full), ((1,), (1,)))
        value = value + dot(up_grad, pick(up_full), ((1,), (1,)))
        return value.astype(jnp.bfloat16).reshape(rows, N_Y, width).transpose(1, 0, 2)

    from_core = send_core(half_partial(1 - core))
    pair_sum = add(half_partial(core), from_core).astype(jnp.bfloat16)
    summed = lax.all_to_all(pair_sum, "mp", 0, 0, axis_index_groups=Y_GROUPS)

    down_z = lax.psum_scatter(
        down_partial, "fsdp", scatter_dimension=0, axis_index_groups=Z_GROUPS, tiled=True
    ).reshape(N_X, depth, cols)
    down_sum = lax.dynamic_index_in_dim(down_z, me_x, 0, False).astype(jnp.float32)
    for step in (1, N_X - 1, 2):
        block = lax.dynamic_index_in_dim(down_z, (me_x + step) % N_X, 0, False)
        down_sum = down_sum + send_x(block, step).astype(jnp.float32)
    grad_down = (down_sum * factor).astype(jnp.bfloat16)
    input_grad = summed.astype(jnp.float32).sum(0).astype(jnp.bfloat16)
    return (input_grad, grad_down)


def solution(mesh):
    placed = P("fsdp", "mp")
    return jax.shard_map(
        on_device,
        mesh=mesh,
        in_specs=(placed,) * 5,
        out_specs=(placed, placed),
        check_vma=False,
    )
```

```python
import math

import jax
import jax.numpy as jnp
from jax import lax
from jax.experimental import pallas as pl
from jax.experimental.pallas import tpu as pltpu
from jax.sharding import PartitionSpec as P

N_Z = 8
N_X = 4
N_Y = 8
N_CORE = 2
Z_GROUPS = [[z * N_X + x for z in range(N_Z)] for x in range(N_X)]
X_GROUPS = [[z * N_X + x for x in range(N_X)] for z in range(N_Z)]
Y_GROUPS = [[y * N_CORE + c for y in range(N_Y)] for c in range(N_CORE)]


def dot(left, right, dims):
    return lax.dot_general(left, right, (dims, ((), ())), preferred_element_type=jnp.float32)


def copy_blocks(blocks, full, sems, me_x):
    depth = blocks[0].shape[1]
    copies = []
    for i, step in enumerate((0, N_X - 1, 1, 2)):
        x = lax.rem(me_x + step, N_X)
        row = pl.multiple_of(lax.rem(x, 2) * depth, depth)
        target = full.at[:, lax.div(x, 2), pl.ds(row, depth), :]
        copies.append(pltpu.make_async_copy(blocks[i], target, sems.at[i]))
    for copy in copies:
        copy.start()
    return copies


def forward_kernel(
    place, rows_ref, g0, g1, g2, g3, u0, u1, u2, u3, gate_out, up_out, partial_out,
    tok, cot, gate_full, up_full, row_sems, gate_sems, up_sems,
):
    me_x = place[0]
    count = tok.shape[0]
    tok_copy = pltpu.make_async_copy(rows_ref.at[pl.ds(0, count)], tok, row_sems.at[0])
    cot_copy = pltpu.make_async_copy(rows_ref.at[pl.ds(count, count)], cot, row_sems.at[1])
    tok_copy.start()
    gate_copies = copy_blocks((g0, g1, g2, g3), gate_full, gate_sems, me_x)
    up_copies = copy_blocks((u0, u1, u2, u3), up_full, up_sems, me_x)
    cot_copy.start()
    n_feat, cols = partial_out.shape
    tok_copy.wait()
    for copy in gate_copies:
        copy.wait()
    gate_value = jnp.dot(
        tok[...], gate_full[...].reshape(n_feat, cols), preferred_element_type=jnp.float32
    )
    gate_out[...] = gate_value
    for copy in up_copies:
        copy.wait()
    up_value = jnp.dot(
        tok[...], up_full[...].reshape(n_feat, cols), preferred_element_type=jnp.float32
    )
    up_out[...] = up_value
    hidden = (gate_value * jax.nn.sigmoid(gate_value) * up_value).astype(jnp.bfloat16)
    cot_copy.wait()
    partial_out[...] = dot(cot[...], hidden, ((0,), (0,))).astype(jnp.bfloat16)


def backward_kernel(
    place, rows_ref, down_ref, g0, g1, g2, g3, u0, u1, u2, u3, gate_in, up_in, other_out, mine_out,
    cot, down_full, gate_full, up_full, row_sem, down_sem, gate_sems, up_sems,
):
    me_x, core = place[0], place[1]
    count = cot.shape[0]
    n_z, _, wide, cols = gate_full.shape
    cot_copy = pltpu.make_async_copy(rows_ref.at[pl.ds(count, count)], cot, row_sem.at[0])
    down_copy = pltpu.make_async_copy(down_ref, down_full, down_sem.at[0])
    cot_copy.start()
    down_copy.start()
    gate_copies = copy_blocks((g0, g1, g2, g3), gate_full, gate_sems, me_x)
    up_copies = copy_blocks((u0, u1, u2, u3), up_full, up_sems, me_x)
    gate_value, up_value = gate_in[...], up_in[...]
    sigmoid_gate = jax.nn.sigmoid(gate_value)
    cot_copy.wait()
    down_copy.wait()
    hidden_grad = jnp.dot(
        cot[...], down_full[...].reshape(-1, cols), preferred_element_type=jnp.float32
    )
    gate_grad = (
        hidden_grad * up_value * sigmoid_gate * (1.0 + gate_value * (1.0 - sigmoid_gate))
    ).astype(jnp.bfloat16)
    up_grad = (hidden_grad * gate_value * sigmoid_gate).astype(jnp.bfloat16)
    grads = jnp.concatenate([gate_grad, up_grad], axis=1)
    for copy in gate_copies + up_copies:
        copy.wait()
    for out, which in ((other_out, 1 - core), (mine_out, core)):
        for y in range(0, n_z, 2):
            pair = [
                jnp.concatenate([gate_full[y + i, which], up_full[y + i, which]], axis=1)
                for i in range(2)
            ]
            value = dot(grads, jnp.concatenate(pair), ((1,), (1,))).astype(jnp.bfloat16)
            out[y] = value[:, :wide]
            out[y + 1] = value[:, wide:]


def call_kernel(kernel, n_smem_any, operands, out_shapes, scratch, flops):
    in_specs = [pl.BlockSpec(memory_space=pltpu.SMEM)]
    in_specs += [pl.BlockSpec(memory_space=pl.ANY)] * n_smem_any
    in_specs += [pl.BlockSpec(memory_space=pltpu.VMEM)] * (len(operands) - 1 - n_smem_any)
    return pl.pallas_call(
        kernel,
        out_shape=out_shapes,
        in_specs=in_specs,
        out_specs=[pl.BlockSpec(memory_space=pltpu.VMEM)] * len(out_shapes),
        scratch_shapes=scratch,
        compiler_params=pltpu.CompilerParams(vmem_limit_bytes=28 * 1024 * 1024),
        cost_estimate=pl.CostEstimate(flops=flops, bytes_accessed=10_000_000, transcendentals=0),
    )(*operands)


def send_x(value, step):
    pairs = [
        (z * N_X + x, z * N_X + (x + step) % N_X) for z in range(N_Z) for x in range(N_X)
    ]
    return lax.ppermute(value, "fsdp", pairs)


def send_core(value):
    pairs = [(i, i ^ 1) for i in range(N_Y * N_CORE)]
    return lax.ppermute(value, "mp", pairs)


def copies_of(block):
    return jnp.broadcast_to(block[None], (N_Z,) + block.shape)


def gather_z(copies):
    return lax.all_to_all(copies, "fsdp", 0, 0, axis_index_groups=Z_GROUPS)


def add(left, right):
    return left.astype(jnp.float32) + right.astype(jnp.float32)


def on_device(tokens, cotangent, gate_weight, up_weight, down_weight):
    n_fsdp = lax.axis_size("fsdp")
    rows, width = tokens.shape
    depth, cols = gate_weight.shape
    n_feat = depth * n_fsdp
    factor = 1.0 / math.sqrt(rows * n_fsdp)
    me_x = lax.axis_index("fsdp") % N_X
    core = lax.axis_index("mp") % N_CORE

    gate_copies = copies_of(gate_weight)
    gate_copies, tokens, cotangent = lax.optimization_barrier((gate_copies, tokens, cotangent))
    stacked = jnp.concatenate([tokens, cotangent])
    both = lax.all_gather(stacked, "mp", axis=1, tiled=True)

    down_x = jnp.zeros((N_X, depth, cols), down_weight.dtype)
    down_x = lax.dynamic_update_slice(down_x, down_weight[None], (me_x, 0, 0))
    for step in (1, N_X - 1, 2):
        block = send_x(down_weight, step)
        down_x = lax.dynamic_update_slice(down_x, block[None], ((me_x - step) % N_X, 0, 0))

    gate_z = gather_z(gate_copies)
    gate_left, gate_right = send_x(gate_z, 1), send_x(gate_z, -1)
    gate_z, up_copies = lax.optimization_barrier((gate_z, copies_of(up_weight)))
    up_z = gather_z(up_copies)
    up_z, down_copies = lax.optimization_barrier((up_z, copies_of(down_x)))
    down_full = gather_z(down_copies).reshape(N_Z, N_CORE, 2 * depth, cols)

    up_z, gate_left, gate_right = lax.optimization_barrier((up_z, gate_left, gate_right))
    up_right, up_left = send_x(up_z, -1), send_x(up_z, 1)
    gate_far, up_far = send_x(gate_left, 1), send_x(up_right, -1)
    blocks = (gate_z, gate_left, gate_right, gate_far, up_z, up_left, up_right, up_far)

    place = jnp.stack([me_x, core]).astype(jnp.int32)
    value = jax.ShapeDtypeStruct((rows, cols), jnp.float32)
    full = pltpu.VMEM((N_Z, N_CORE, 2 * depth, cols), jnp.bfloat16)
    row_block = pltpu.VMEM((rows, n_feat), jnp.bfloat16)
    sems = pltpu.SemaphoreType.DMA
    gate_value, up_value, down_partial = call_kernel(
        forward_kernel,
        9,
        (place, both) + blocks,
        (value, value, jax.ShapeDtypeStruct((n_feat, cols), jnp.bfloat16)),
        [row_block, row_block, full, full, sems((2,)), sems((N_X,)), sems((N_X,))],
        6 * rows * n_feat * cols,
    )
    half = jax.ShapeDtypeStruct((N_Y, rows, width), jnp.bfloat16)
    other, mine = call_kernel(
        backward_kernel,
        10,
        (place, both, down_full) + blocks + (gate_value, up_value),
        (half, half),
        [row_block, full, full, full, sems((1,)), sems((1,)), sems((N_X,)), sems((N_X,))],
        6 * rows * n_feat * cols,
    )
    pair_sum = add(mine, send_core(other)).astype(jnp.bfloat16)
    summed = lax.all_to_all(pair_sum, "mp", 0, 0, axis_index_groups=Y_GROUPS)

    down_z = lax.psum_scatter(
        down_partial, "fsdp", scatter_dimension=0, axis_index_groups=Z_GROUPS, tiled=True
    ).reshape(N_X, depth, cols)
    down_sum = lax.dynamic_index_in_dim(down_z, me_x, 0, False).astype(jnp.float32)
    for step in (1, N_X - 1, 2):
        block = lax.dynamic_index_in_dim(down_z, (me_x + step) % N_X, 0, False)
        down_sum = down_sum + send_x(block, step).astype(jnp.float32)
    grad_down = (down_sum * factor).astype(jnp.bfloat16)
    input_grad = summed.astype(jnp.float32).sum(0).astype(jnp.bfloat16)
    return (input_grad, grad_down)


def solution(mesh):
    placed = P("fsdp", "mp")
    return jax.shard_map(
        on_device,
        mesh=mesh,
        in_specs=(placed,) * 5,
        out_specs=(placed, placed),
        check_vma=False,
    )
```

```python
import math

import jax
import jax.numpy as jnp
from jax import lax
from jax.experimental import pallas as pl
from jax.experimental.pallas import tpu as pltpu
from jax.sharding import PartitionSpec as P

N_Z = 8
N_X = 4
N_Y = 8
N_CORE = 2
Z_GROUPS = [[z * N_X + x for z in range(N_Z)] for x in range(N_X)]
X_GROUPS = [[z * N_X + x for x in range(N_X)] for z in range(N_Z)]
Y_GROUPS = [[y * N_CORE + c for y in range(N_Y)] for c in range(N_CORE)]


def dot(left, right, dims):
    return lax.dot_general(left, right, (dims, ((), ())), preferred_element_type=jnp.float32)


def copy_blocks(blocks, full, sems, me_x):
    depth = blocks[0].shape[1]
    copies = []
    for i, step in enumerate((0, N_X - 1, 1, 2)):
        x = lax.rem(me_x + step, N_X)
        row = pl.multiple_of(lax.rem(x, 2) * depth, depth)
        target = full.at[:, lax.div(x, 2), pl.ds(row, depth), :]
        copies.append(pltpu.make_async_copy(blocks[i], target, sems.at[i]))
    for copy in copies:
        copy.start()
    return copies


def forward_kernel(
    place, rows_ref, g0, g1, g2, g3, u0, u1, u2, u3, gate_out, up_out, partial_out,
    tok, cot, gate_full, up_full, row_sems, gate_sems, up_sems,
):
    me_x = place[0]
    count = tok.shape[0]
    tok_copy = pltpu.make_async_copy(rows_ref.at[pl.ds(0, count)], tok, row_sems.at[0])
    cot_copy = pltpu.make_async_copy(rows_ref.at[pl.ds(count, count)], cot, row_sems.at[1])
    tok_copy.start()
    gate_copies = copy_blocks((g0, g1, g2, g3), gate_full, gate_sems, me_x)
    up_copies = copy_blocks((u0, u1, u2, u3), up_full, up_sems, me_x)
    cot_copy.start()
    n_feat, cols = partial_out.shape
    tok_copy.wait()
    for copy in gate_copies:
        copy.wait()
    gate_value = jnp.dot(
        tok[...], gate_full[...].reshape(n_feat, cols), preferred_element_type=jnp.float32
    )
    gate_out[...] = gate_value
    for copy in up_copies:
        copy.wait()
    up_value = jnp.dot(
        tok[...], up_full[...].reshape(n_feat, cols), preferred_element_type=jnp.float32
    )
    up_out[...] = up_value
    hidden = (gate_value * jax.nn.sigmoid(gate_value) * up_value).astype(jnp.bfloat16)
    cot_copy.wait()
    partial_out[...] = dot(cot[...], hidden, ((0,), (0,))).astype(jnp.bfloat16)


def backward_kernel(
    place, rows_ref, down_ref, g0, g1, g2, g3, u0, u1, u2, u3, gate_in, up_in, other_out, mine_out,
    cot, down_full, gate_full, up_full, row_sem, down_sem, gate_sems, up_sems,
):
    me_x, core = place[0], place[1]
    count = cot.shape[0]
    n_z, _, wide, cols = gate_full.shape
    cot_copy = pltpu.make_async_copy(rows_ref.at[pl.ds(count, count)], cot, row_sem.at[0])
    down_copy = pltpu.make_async_copy(down_ref, down_full, down_sem.at[0])
    cot_copy.start()
    down_copy.start()
    gate_copies = copy_blocks((g0, g1, g2, g3), gate_full, gate_sems, me_x)
    up_copies = copy_blocks((u0, u1, u2, u3), up_full, up_sems, me_x)
    gate_value, up_value = gate_in[...], up_in[...]
    sigmoid_gate = jax.nn.sigmoid(gate_value)
    cot_copy.wait()
    down_copy.wait()
    hidden_grad = jnp.dot(
        cot[...], down_full[...].reshape(-1, cols), preferred_element_type=jnp.float32
    )
    gate_grad = (
        hidden_grad * up_value * sigmoid_gate * (1.0 + gate_value * (1.0 - sigmoid_gate))
    ).astype(jnp.bfloat16)
    up_grad = (hidden_grad * gate_value * sigmoid_gate).astype(jnp.bfloat16)
    grads = jnp.concatenate([gate_grad, up_grad], axis=1)
    for copy in gate_copies + up_copies:
        copy.wait()
    for out, which in ((other_out, 1 - core), (mine_out, core)):
        for y in range(0, n_z, 2):
            pair = [
                jnp.concatenate([gate_full[y + i, which], up_full[y + i, which]], axis=1)
                for i in range(2)
            ]
            value = dot(grads, jnp.concatenate(pair), ((1,), (1,))).astype(jnp.bfloat16)
            out[y] = value[:, :wide]
            out[y + 1] = value[:, wide:]


def call_kernel(kernel, n_smem_any, operands, out_shapes, scratch, flops):
    in_specs = [pl.BlockSpec(memory_space=pltpu.SMEM)]
    in_specs += [pl.BlockSpec(memory_space=pl.ANY)] * n_smem_any
    in_specs += [pl.BlockSpec(memory_space=pltpu.VMEM)] * (len(operands) - 1 - n_smem_any)
    return pl.pallas_call(
        kernel,
        out_shape=out_shapes,
        in_specs=in_specs,
        out_specs=[pl.BlockSpec(memory_space=pltpu.VMEM)] * len(out_shapes),
        scratch_shapes=scratch,
        compiler_params=pltpu.CompilerParams(vmem_limit_bytes=60 * 1024 * 1024),
        cost_estimate=pl.CostEstimate(flops=flops, bytes_accessed=10_000_000, transcendentals=0),
    )(*operands)


def send_x(value, step):
    pairs = [
        (z * N_X + x, z * N_X + (x + step) % N_X) for z in range(N_Z) for x in range(N_X)
    ]
    return lax.ppermute(value, "fsdp", pairs)


def send_core(value):
    pairs = [(i, i ^ 1) for i in range(N_Y * N_CORE)]
    return lax.ppermute(value, "mp", pairs)


def copies_of(block):
    return jnp.broadcast_to(block[None], (N_Z,) + block.shape)


def gather_z(copies):
    return lax.all_to_all(copies, "fsdp", 0, 0, axis_index_groups=Z_GROUPS)


def add(left, right):
    return left.astype(jnp.float32) + right.astype(jnp.float32)


def on_device(tokens, cotangent, gate_weight, up_weight, down_weight):
    n_fsdp = lax.axis_size("fsdp")
    rows, width = tokens.shape
    depth, cols = gate_weight.shape
    n_feat = depth * n_fsdp
    factor = 1.0 / math.sqrt(rows * n_fsdp)
    me_x = lax.axis_index("fsdp") % N_X
    core = lax.axis_index("mp") % N_CORE

    gate_copies = copies_of(gate_weight)
    gate_copies, tokens, cotangent = lax.optimization_barrier((gate_copies, tokens, cotangent))
    stacked = jnp.concatenate([tokens, cotangent])
    both = lax.all_gather(stacked, "mp", axis=1, tiled=True)

    down_x = jnp.zeros((N_X, depth, cols), down_weight.dtype)
    down_x = lax.dynamic_update_slice(down_x, down_weight[None], (me_x, 0, 0))
    for step in (1, N_X - 1, 2):
        block = send_x(down_weight, step)
        down_x = lax.dynamic_update_slice(down_x, block[None], ((me_x - step) % N_X, 0, 0))

    gate_z = gather_z(gate_copies)
    gate_left, gate_right = send_x(gate_z, 1), send_x(gate_z, -1)
    gate_z, up_copies = lax.optimization_barrier((gate_z, copies_of(up_weight)))
    up_z = gather_z(up_copies)
    up_z, down_copies, gate_left = lax.optimization_barrier((up_z, copies_of(down_x), gate_left))
    down_full = gather_z(down_copies).reshape(N_Z, N_CORE, 2 * depth, cols)

    up_right, up_left = send_x(up_z, -1), send_x(up_z, 1)
    gate_far, up_far = send_x(gate_left, 1), send_x(up_right, -1)
    blocks = (gate_z, gate_left, gate_right, gate_far, up_z, up_left, up_right, up_far)

    place = jnp.stack([me_x, core]).astype(jnp.int32)
    value = jax.ShapeDtypeStruct((rows, cols), jnp.float32)
    full = pltpu.VMEM((N_Z, N_CORE, 2 * depth, cols), jnp.bfloat16)
    row_block = pltpu.VMEM((rows, n_feat), jnp.bfloat16)
    sems = pltpu.SemaphoreType.DMA
    gate_value, up_value, down_partial = call_kernel(
        forward_kernel,
        9,
        (place, both) + blocks,
        (value, value, jax.ShapeDtypeStruct((n_feat, cols), jnp.bfloat16)),
        [row_block, row_block, full, full, sems((2,)), sems((N_X,)), sems((N_X,))],
        6 * rows * n_feat * cols,
    )
    half = jax.ShapeDtypeStruct((N_Y, rows, width), jnp.bfloat16)
    other, mine = call_kernel(
        backward_kernel,
        10,
        (place, both, down_full) + blocks + (gate_value, up_value),
        (half, half),
        [row_block, full, full, full, sems((1,)), sems((1,)), sems((N_X,)), sems((N_X,))],
        6 * rows * n_feat * cols,
    )
    pair_sum = add(mine, send_core(other)).astype(jnp.bfloat16)
    summed = lax.all_to_all(pair_sum, "mp", 0, 0, axis_index_groups=Y_GROUPS)

    down_z = lax.psum_scatter(
        down_partial, "fsdp", scatter_dimension=0, axis_index_groups=Z_GROUPS, tiled=True
    ).reshape(N_X, depth, cols)
    down_sum = lax.dynamic_index_in_dim(down_z, me_x, 0, False).astype(jnp.float32)
    for step in (1, N_X - 1, 2):
        block = lax.dynamic_index_in_dim(down_z, (me_x + step) % N_X, 0, False)
        down_sum = down_sum + send_x(block, step).astype(jnp.float32)
    grad_down = (down_sum * factor).astype(jnp.bfloat16)
    input_grad = summed.astype(jnp.float32).sum(0).astype(jnp.bfloat16)
    return (input_grad, grad_down)


def solution(mesh):
    placed = P("fsdp", "mp")
    return jax.shard_map(
        on_device,
        mesh=mesh,
        in_specs=(placed,) * 5,
        out_specs=(placed, placed),
        check_vma=False,
    )
```

```python
import math

import jax
import jax.numpy as jnp
from jax import lax
from jax.experimental import pallas as pl
from jax.experimental.pallas import tpu as pltpu
from jax.sharding import PartitionSpec as P

N_Z = 8
N_X = 4
N_Y = 8
N_CORE = 2
Z_GROUPS = [[z * N_X + x for z in range(N_Z)] for x in range(N_X)]
X_GROUPS = [[z * N_X + x for x in range(N_X)] for z in range(N_Z)]
Y_GROUPS = [[y * N_CORE + c for y in range(N_Y)] for c in range(N_CORE)]


def dot(left, right, dims):
    return lax.dot_general(left, right, (dims, ((), ())), preferred_element_type=jnp.float32)


def copy_blocks(blocks, full, sems, me_x):
    depth = blocks[0].shape[1]
    copies = []
    for i, step in enumerate((0, N_X - 1, 1, 2)):
        x = lax.rem(me_x + step, N_X)
        row = pl.multiple_of(lax.rem(x, 2) * depth, depth)
        target = full.at[:, lax.div(x, 2), pl.ds(row, depth), :]
        copies.append(pltpu.make_async_copy(blocks[i], target, sems.at[i]))
    for copy in copies:
        copy.start()
    return copies


def gate_kernel(place, rows_ref, g0, g1, g2, g3, gate_out, tok, gate_full, row_sem, gate_sems):
    count, n_feat = tok.shape
    tok_copy = pltpu.make_async_copy(rows_ref.at[pl.ds(0, count)], tok, row_sem.at[0])
    tok_copy.start()
    gate_copies = copy_blocks((g0, g1, g2, g3), gate_full, gate_sems, place[0])
    tok_copy.wait()
    for copy in gate_copies:
        copy.wait()
    gate_out[...] = jnp.dot(
        tok[...], gate_full[...].reshape(n_feat, -1), preferred_element_type=jnp.float32
    )


def forward_kernel(
    place, rows_ref, u0, u1, u2, u3, gate_in, up_out, partial_out,
    tok, cot, up_full, row_sems, up_sems,
):
    count, n_feat = tok.shape
    tok_copy = pltpu.make_async_copy(rows_ref.at[pl.ds(0, count)], tok, row_sems.at[0])
    cot_copy = pltpu.make_async_copy(rows_ref.at[pl.ds(count, count)], cot, row_sems.at[1])
    tok_copy.start()
    up_copies = copy_blocks((u0, u1, u2, u3), up_full, up_sems, place[0])
    cot_copy.start()
    gate_value = gate_in[...]
    silu = gate_value * jax.nn.sigmoid(gate_value)
    tok_copy.wait()
    for copy in up_copies:
        copy.wait()
    up_value = jnp.dot(
        tok[...], up_full[...].reshape(n_feat, -1), preferred_element_type=jnp.float32
    )
    up_out[...] = up_value
    hidden = (silu * up_value).astype(jnp.bfloat16)
    cot_copy.wait()
    partial_out[...] = dot(cot[...], hidden, ((0,), (0,))).astype(jnp.bfloat16)


def backward_kernel(
    place, rows_ref, down_ref, g0, g1, g2, g3, u0, u1, u2, u3, gate_in, up_in, other_out, mine_out,
    cot, down_full, gate_full, up_full, row_sem, down_sem, gate_sems, up_sems,
):
    me_x, core = place[0], place[1]
    count = cot.shape[0]
    n_z, _, wide, cols = gate_full.shape
    cot_copy = pltpu.make_async_copy(rows_ref.at[pl.ds(count, count)], cot, row_sem.at[0])
    down_copy = pltpu.make_async_copy(down_ref, down_full, down_sem.at[0])
    cot_copy.start()
    down_copy.start()
    gate_copies = copy_blocks((g0, g1, g2, g3), gate_full, gate_sems, me_x)
    up_copies = copy_blocks((u0, u1, u2, u3), up_full, up_sems, me_x)
    gate_value, up_value = gate_in[...], up_in[...]
    sigmoid_gate = jax.nn.sigmoid(gate_value)
    cot_copy.wait()
    down_copy.wait()
    hidden_grad = jnp.dot(
        cot[...], down_full[...].reshape(-1, cols), preferred_element_type=jnp.float32
    )
    gate_grad = (
        hidden_grad * up_value * sigmoid_gate * (1.0 + gate_value * (1.0 - sigmoid_gate))
    ).astype(jnp.bfloat16)
    up_grad = (hidden_grad * gate_value * sigmoid_gate).astype(jnp.bfloat16)
    grads = jnp.concatenate([gate_grad, up_grad], axis=1)
    for copy in gate_copies + up_copies:
        copy.wait()
    for out, which in ((other_out, 1 - core), (mine_out, core)):
        for y in range(0, n_z, 2):
            pair = [
                jnp.concatenate([gate_full[y + i, which], up_full[y + i, which]], axis=1)
                for i in range(2)
            ]
            value = dot(grads, jnp.concatenate(pair), ((1,), (1,))).astype(jnp.bfloat16)
            out[y] = value[:, :wide]
            out[y + 1] = value[:, wide:]


def call_kernel(kernel, n_smem_any, operands, out_shapes, scratch, flops):
    in_specs = [pl.BlockSpec(memory_space=pltpu.SMEM)]
    in_specs += [pl.BlockSpec(memory_space=pl.ANY)] * n_smem_any
    in_specs += [pl.BlockSpec(memory_space=pltpu.VMEM)] * (len(operands) - 1 - n_smem_any)
    return pl.pallas_call(
        kernel,
        out_shape=out_shapes,
        in_specs=in_specs,
        out_specs=[pl.BlockSpec(memory_space=pltpu.VMEM)] * len(out_shapes),
        scratch_shapes=scratch,
        compiler_params=pltpu.CompilerParams(vmem_limit_bytes=60 * 1024 * 1024),
        cost_estimate=pl.CostEstimate(flops=flops, bytes_accessed=10_000_000, transcendentals=0),
    )(*operands)


def send_x(value, step):
    pairs = [
        (z * N_X + x, z * N_X + (x + step) % N_X) for z in range(N_Z) for x in range(N_X)
    ]
    return lax.ppermute(value, "fsdp", pairs)


def swap_x(value, flip):
    pairs = [(z * N_X + x, z * N_X + (x ^ flip)) for z in range(N_Z) for x in range(N_X)]
    return lax.ppermute(value, "fsdp", pairs)


def send_core(value):
    pairs = [(i, i ^ 1) for i in range(N_Y * N_CORE)]
    return lax.ppermute(value, "mp", pairs)


def copies_of(block):
    return jnp.broadcast_to(block[None], (N_Z,) + block.shape)


def gather_z(copies):
    return lax.all_to_all(copies, "fsdp", 0, 0, axis_index_groups=Z_GROUPS)


def add(left, right):
    return left.astype(jnp.float32) + right.astype(jnp.float32)


def on_device(tokens, cotangent, gate_weight, up_weight, down_weight):
    n_fsdp = lax.axis_size("fsdp")
    rows, width = tokens.shape
    depth, cols = gate_weight.shape
    n_feat = depth * n_fsdp
    factor = 1.0 / math.sqrt(rows * n_fsdp)
    me_x = lax.axis_index("fsdp") % N_X
    core = lax.axis_index("mp") % N_CORE

    gate_copies = copies_of(gate_weight)
    gate_copies, tokens, cotangent = lax.optimization_barrier((gate_copies, tokens, cotangent))
    stacked = jnp.concatenate([tokens, cotangent])
    both = lax.all_gather(stacked, "mp", axis=1, tiled=True)

    down_x = jnp.zeros((N_X, depth, cols), down_weight.dtype)
    down_x = lax.dynamic_update_slice(down_x, down_weight[None], (me_x, 0, 0))
    for step in (1, N_X - 1, 2):
        block = send_x(down_weight, step)
        down_x = lax.dynamic_update_slice(down_x, block[None], ((me_x - step) % N_X, 0, 0))

    gate_z = gather_z(gate_copies)
    gate_left, gate_right = send_x(gate_z, 1), send_x(gate_z, -1)
    gate_z, up_copies = lax.optimization_barrier((gate_z, copies_of(up_weight)))
    up_z = gather_z(up_copies)
    up_z, down_copies, gate_left, gate_right = lax.optimization_barrier(
        (up_z, copies_of(down_x), gate_left, gate_right)
    )
    down_full = gather_z(down_copies).reshape(N_Z, N_CORE, 2 * depth, cols)

    up_right, up_left = send_x(up_z, -1), send_x(up_z, 1)
    gate_far, up_far = send_x(gate_left, 1), send_x(up_right, -1)
    blocks = (gate_z, gate_left, gate_right, gate_far, up_z, up_left, up_right, up_far)

    place = jnp.stack([me_x, core]).astype(jnp.int32)
    value = jax.ShapeDtypeStruct((rows, cols), jnp.float32)
    full = pltpu.VMEM((N_Z, N_CORE, 2 * depth, cols), jnp.bfloat16)
    row_block = pltpu.VMEM((rows, n_feat), jnp.bfloat16)
    sems = pltpu.SemaphoreType.DMA
    (gate_value,) = call_kernel(
        gate_kernel,
        5,
        (place, both) + blocks[:4],
        (value,),
        [row_block, full, sems((1,)), sems((N_X,))],
        2 * rows * n_feat * cols,
    )
    up_value, down_partial = call_kernel(
        forward_kernel,
        5,
        (place, both) + blocks[4:] + (gate_value,),
        (value, jax.ShapeDtypeStruct((n_feat, cols), jnp.bfloat16)),
        [row_block, row_block, full, sems((2,)), sems((N_X,))],
        4 * rows * n_feat * cols,
    )
    half = jax.ShapeDtypeStruct((N_Y, rows, width), jnp.bfloat16)
    other, mine = call_kernel(
        backward_kernel,
        10,
        (place, both, down_full) + blocks + (gate_value, up_value),
        (half, half),
        [row_block, full, full, full, sems((1,)), sems((1,)), sems((N_X,)), sems((N_X,))],
        6 * rows * n_feat * cols,
    )
    pair_sum = add(mine, send_core(other)).astype(jnp.bfloat16)
    summed = lax.all_to_all(pair_sum, "mp", 0, 0, axis_index_groups=Y_GROUPS)

    down_z = lax.psum_scatter(
        down_partial, "fsdp", scatter_dimension=0, axis_index_groups=Z_GROUPS, tiled=True
    ).reshape(N_X, depth, cols)
    block = lambda flip: lax.dynamic_index_in_dim(down_z, me_x ^ flip, 0, False)
    received = swap_x(jnp.stack([block(1), block(2)]), 1)
    passed = swap_x(add(block(3), received[1]).astype(jnp.bfloat16), 3)
    down_sum = add(block(0), received[0]) + passed.astype(jnp.float32)
    grad_down = (down_sum * factor).astype(jnp.bfloat16)
    input_grad = summed.astype(jnp.float32).sum(0).astype(jnp.bfloat16)
    return (input_grad, grad_down)


def solution(mesh):
    placed = P("fsdp", "mp")
    return jax.shard_map(
        on_device,
        mesh=mesh,
        in_specs=(placed,) * 5,
        out_specs=(placed, placed),
        check_vma=False,
    )
```

```python
import math

import jax
import jax.numpy as jnp
from jax import lax
from jax.experimental import pallas as pl
from jax.experimental.pallas import tpu as pltpu
from jax.sharding import PartitionSpec as P

N_Z = 8
N_X = 4
N_Y = 8
N_CORE = 2
Z_GROUPS = [[z * N_X + x for z in range(N_Z)] for x in range(N_X)]
Y_GROUPS = [[y * N_CORE + c for y in range(N_Y)] for c in range(N_CORE)]


def dot(left, right, dims):
    return lax.dot_general(left, right, (dims, ((), ())), preferred_element_type=jnp.float32)


def copy_blocks(blocks, full, sems, me_x):
    depth = blocks[0].shape[1]
    copies = []
    for i, step in enumerate((0, N_X - 1, 1, 2)):
        x = lax.rem(me_x + step, N_X)
        row = pl.multiple_of(lax.rem(x, 2) * depth, depth)
        target = full.at[:, lax.div(x, 2), pl.ds(row, depth), :]
        copies.append(pltpu.make_async_copy(blocks[i], target, sems.at[i]))
    for copy in copies:
        copy.start()
    return copies


def gate_kernel(place, rows_ref, g0, g1, g2, g3, gate_out, tok, gate_full, row_sem, gate_sems):
    count, n_feat = tok.shape
    tok_copy = pltpu.make_async_copy(rows_ref.at[pl.ds(0, count)], tok, row_sem.at[0])
    tok_copy.start()
    gate_copies = copy_blocks((g0, g1, g2, g3), gate_full, gate_sems, place[0])
    tok_copy.wait()
    for copy in gate_copies:
        copy.wait()
    gate_out[...] = jnp.dot(
        tok[...], gate_full[...].reshape(n_feat, -1), preferred_element_type=jnp.float32
    )


def forward_kernel(
    place, rows_ref, u0, u1, u2, u3, gate_in, up_out, partial_out,
    tok, cot, up_full, row_sems, up_sems,
):
    count, n_feat = tok.shape
    tok_copy = pltpu.make_async_copy(rows_ref.at[pl.ds(0, count)], tok, row_sems.at[0])
    cot_copy = pltpu.make_async_copy(rows_ref.at[pl.ds(count, count)], cot, row_sems.at[1])
    tok_copy.start()
    up_copies = copy_blocks((u0, u1, u2, u3), up_full, up_sems, place[0])
    cot_copy.start()
    gate_value = gate_in[...]
    silu = gate_value * jax.nn.sigmoid(gate_value)
    tok_copy.wait()
    for copy in up_copies:
        copy.wait()
    up_value = jnp.dot(
        tok[...], up_full[...].reshape(n_feat, -1), preferred_element_type=jnp.float32
    )
    up_out[...] = up_value
    hidden = (silu * up_value).astype(jnp.bfloat16)
    cot_copy.wait()
    partial_out[...] = dot(cot[...], hidden, ((0,), (0,))).astype(jnp.bfloat16)


def backward_kernel(
    place, rows_ref, down_ref, g0, g1, g2, g3, u0, u1, u2, u3, gate_in, up_in, other_out, mine_out,
    cot, down_full, gate_full, up_full, row_sem, down_sem, gate_sems, up_sems,
):
    me_x, core = place[0], place[1]
    count = cot.shape[0]
    n_z, _, wide, cols = gate_full.shape
    cot_copy = pltpu.make_async_copy(rows_ref.at[pl.ds(count, count)], cot, row_sem.at[0])
    down_copy = pltpu.make_async_copy(down_ref, down_full, down_sem.at[0])
    cot_copy.start()
    down_copy.start()
    gate_copies = copy_blocks((g0, g1, g2, g3), gate_full, gate_sems, me_x)
    up_copies = copy_blocks((u0, u1, u2, u3), up_full, up_sems, me_x)
    gate_value, up_value = gate_in[...], up_in[...]
    sigmoid_gate = jax.nn.sigmoid(gate_value)
    cot_copy.wait()
    down_copy.wait()
    hidden_grad = jnp.dot(
        cot[...], down_full[...].reshape(-1, cols), preferred_element_type=jnp.float32
    )
    gate_grad = (
        hidden_grad * up_value * sigmoid_gate * (1.0 + gate_value * (1.0 - sigmoid_gate))
    ).astype(jnp.bfloat16)
    up_grad = (hidden_grad * gate_value * sigmoid_gate).astype(jnp.bfloat16)
    grads = jnp.concatenate([gate_grad, up_grad], axis=1)
    for copy in gate_copies + up_copies:
        copy.wait()
    for out, which in ((other_out, 1 - core), (mine_out, core)):
        for y in range(0, n_z, 2):
            pair = [
                jnp.concatenate([gate_full[y + i, which], up_full[y + i, which]], axis=1)
                for i in range(2)
            ]
            value = dot(grads, jnp.concatenate(pair), ((1,), (1,))).astype(jnp.bfloat16)
            out[y] = value[:, :wide]
            out[y + 1] = value[:, wide:]


def call_kernel(kernel, n_smem_any, operands, out_shapes, scratch, flops):
    in_specs = [pl.BlockSpec(memory_space=pltpu.SMEM)]
    in_specs += [pl.BlockSpec(memory_space=pl.ANY)] * n_smem_any
    in_specs += [pl.BlockSpec(memory_space=pltpu.VMEM)] * (len(operands) - 1 - n_smem_any)
    return pl.pallas_call(
        kernel,
        out_shape=out_shapes,
        in_specs=in_specs,
        out_specs=[pl.BlockSpec(memory_space=pltpu.VMEM)] * len(out_shapes),
        scratch_shapes=scratch,
        compiler_params=pltpu.CompilerParams(vmem_limit_bytes=60 * 1024 * 1024),
        cost_estimate=pl.CostEstimate(flops=flops, bytes_accessed=10_000_000, transcendentals=0),
    )(*operands)


def send_x(value, step):
    pairs = [
        (z * N_X + x, z * N_X + (x + step) % N_X) for z in range(N_Z) for x in range(N_X)
    ]
    return lax.ppermute(value, "fsdp", pairs)


def send_core(value):
    pairs = [(i, i ^ 1) for i in range(N_Y * N_CORE)]
    return lax.ppermute(value, "mp", pairs)


def copies_of(block):
    return jnp.broadcast_to(block[None], (N_Z,) + block.shape)


def gather_z(copies):
    return lax.all_to_all(copies, "fsdp", 0, 0, axis_index_groups=Z_GROUPS)


def add(left, right):
    return left.astype(jnp.float32) + right.astype(jnp.float32)


def on_device(tokens, cotangent, gate_weight, up_weight, down_weight):
    n_fsdp = lax.axis_size("fsdp")
    rows, width = tokens.shape
    depth, cols = gate_weight.shape
    n_feat = depth * n_fsdp
    factor = 1.0 / math.sqrt(rows * n_fsdp)
    me_x = lax.axis_index("fsdp") % N_X
    core = lax.axis_index("mp") % N_CORE

    gate_copies = copies_of(gate_weight)
    gate_copies, tokens, cotangent = lax.optimization_barrier((gate_copies, tokens, cotangent))
    stacked = jnp.concatenate([tokens, cotangent])
    both = lax.all_gather(stacked, "mp", axis=1, tiled=True)

    down_x = jnp.zeros((N_X, depth, cols), down_weight.dtype)
    down_x = lax.dynamic_update_slice(down_x, down_weight[None], (me_x, 0, 0))
    for step in (1, N_X - 1, 2):
        block = send_x(down_weight, step)
        down_x = lax.dynamic_update_slice(down_x, block[None], ((me_x - step) % N_X, 0, 0))

    gate_z = gather_z(gate_copies)
    gate_left, gate_right = send_x(gate_z, 1), send_x(gate_z, -1)
    gate_z, up_copies = lax.optimization_barrier((gate_z, copies_of(up_weight)))
    up_z = gather_z(up_copies)
    up_z, down_copies, gate_left, gate_right = lax.optimization_barrier(
        (up_z, copies_of(down_x), gate_left, gate_right)
    )
    down_full = gather_z(down_copies).reshape(N_Z, N_CORE, 2 * depth, cols)

    up_right, up_left = send_x(up_z, -1), send_x(up_z, 1)
    gate_far, up_far = send_x(gate_left, 1), send_x(up_right, -1)
    blocks = (gate_z, gate_left, gate_right, gate_far, up_z, up_left, up_right, up_far)

    place = jnp.stack([me_x, core]).astype(jnp.int32)
    value = jax.ShapeDtypeStruct((rows, cols), jnp.float32)
    full = pltpu.VMEM((N_Z, N_CORE, 2 * depth, cols), jnp.bfloat16)
    row_block = pltpu.VMEM((rows, n_feat), jnp.bfloat16)
    sems = pltpu.SemaphoreType.DMA
    (gate_value,) = call_kernel(
        gate_kernel,
        5,
        (place, both) + blocks[:4],
        (value,),
        [row_block, full, sems((1,)), sems((N_X,))],
        2 * rows * n_feat * cols,
    )
    up_value, down_partial = call_kernel(
        forward_kernel,
        5,
        (place, both) + blocks[4:] + (gate_value,),
        (value, jax.ShapeDtypeStruct((n_feat, cols), jnp.bfloat16)),
        [row_block, row_block, full, sems((2,)), sems((N_X,))],
        4 * rows * n_feat * cols,
    )
    half = jax.ShapeDtypeStruct((N_Y, rows, width), jnp.bfloat16)
    other, mine = call_kernel(
        backward_kernel,
        10,
        (place, both, down_full) + blocks + (gate_value, up_value),
        (half, half),
        [row_block, full, full, full, sems((1,)), sems((1,)), sems((N_X,)), sems((N_X,))],
        6 * rows * n_feat * cols,
    )
    pair_sum = add(mine, send_core(other)).astype(jnp.bfloat16)
    input_grad = lax.psum_scatter(
        pair_sum.reshape(N_Y * rows, width),
        "mp",
        scatter_dimension=0,
        axis_index_groups=Y_GROUPS,
        tiled=True,
    )
    down_blocks = lax.all_to_all(down_partial.reshape(n_fsdp, depth, cols), "fsdp", 0, 0)
    grad_down = (down_blocks.astype(jnp.float32).sum(0) * factor).astype(jnp.bfloat16)
    return (input_grad, grad_down)


def solution(mesh):
    placed = P("fsdp", "mp")
    return jax.shard_map(
        on_device,
        mesh=mesh,
        in_specs=(placed,) * 5,
        out_specs=(placed, placed),
        check_vma=False,
    )
```

```python
import math

import jax
import jax.numpy as jnp
from jax import lax
from jax.experimental import pallas as pl
from jax.experimental.pallas import tpu as pltpu
from jax.sharding import PartitionSpec as P

N_Z = 8
N_X = 4
N_Y = 8
N_CORE = 2
Z_GROUPS = [[z * N_X + x for z in range(N_Z)] for x in range(N_X)]
X_GROUPS = [[z * N_X + x for x in range(N_X)] for z in range(N_Z)]
Y_GROUPS = [[y * N_CORE + c for y in range(N_Y)] for c in range(N_CORE)]


def dot(left, right, dims):
    return lax.dot_general(left, right, (dims, ((), ())), preferred_element_type=jnp.float32)


def copy_blocks(blocks, full, sems, me_x):
    depth = blocks[0].shape[1]
    copies = []
    for i, step in enumerate((0, N_X - 1, 1, 2)):
        x = lax.rem(me_x + step, N_X)
        row = pl.multiple_of(lax.rem(x, 2) * depth, depth)
        target = full.at[:, lax.div(x, 2), pl.ds(row, depth), :]
        copies.append(pltpu.make_async_copy(blocks[i], target, sems.at[i]))
    for copy in copies:
        copy.start()
    return copies


def gate_kernel(place, rows_ref, g0, g1, g2, g3, gate_out, tok, gate_full, row_sem, gate_sems):
    count, n_feat = tok.shape
    tok_copy = pltpu.make_async_copy(rows_ref.at[pl.ds(0, count)], tok, row_sem.at[0])
    tok_copy.start()
    gate_copies = copy_blocks((g0, g1, g2, g3), gate_full, gate_sems, place[0])
    tok_copy.wait()
    for copy in gate_copies:
        copy.wait()
    gate_out[...] = jnp.dot(
        tok[...], gate_full[...].reshape(n_feat, -1), preferred_element_type=jnp.float32
    )


def forward_kernel(
    place, rows_ref, u0, u1, u2, u3, gate_in, up_out, partial_out,
    tok, cot, up_full, row_sems, up_sems,
):
    count, n_feat = tok.shape
    tok_copy = pltpu.make_async_copy(rows_ref.at[pl.ds(0, count)], tok, row_sems.at[0])
    cot_copy = pltpu.make_async_copy(rows_ref.at[pl.ds(count, count)], cot, row_sems.at[1])
    tok_copy.start()
    up_copies = copy_blocks((u0, u1, u2, u3), up_full, up_sems, place[0])
    cot_copy.start()
    gate_value = gate_in[...]
    silu = gate_value * jax.nn.sigmoid(gate_value)
    tok_copy.wait()
    for copy in up_copies:
        copy.wait()
    up_value = jnp.dot(
        tok[...], up_full[...].reshape(n_feat, -1), preferred_element_type=jnp.float32
    )
    up_out[...] = up_value
    hidden = (silu * up_value).astype(jnp.bfloat16)
    cot_copy.wait()
    partial_value = dot(cot[...], hidden, ((0,), (0,))).astype(jnp.bfloat16)
    depth = n_feat // (N_Z * N_X)
    for z in range(N_Z):
        for x in range(N_X):
            row = (z * N_X + x) * depth
            partial_out[x, z] = partial_value[row : row + depth]


def backward_kernel(
    place, rows_ref, down_ref, g0, g1, g2, g3, u0, u1, u2, u3, gate_in, up_in, other_out, mine_out,
    cot, down_full, gate_full, up_full, row_sem, down_sem, gate_sems, up_sems,
):
    me_x, core = place[0], place[1]
    count = cot.shape[0]
    n_z, _, wide, cols = gate_full.shape
    cot_copy = pltpu.make_async_copy(rows_ref.at[pl.ds(count, count)], cot, row_sem.at[0])
    down_copy = pltpu.make_async_copy(down_ref, down_full, down_sem.at[0])
    cot_copy.start()
    down_copy.start()
    gate_copies = copy_blocks((g0, g1, g2, g3), gate_full, gate_sems, me_x)
    up_copies = copy_blocks((u0, u1, u2, u3), up_full, up_sems, me_x)
    gate_value, up_value = gate_in[...], up_in[...]
    sigmoid_gate = jax.nn.sigmoid(gate_value)
    cot_copy.wait()
    down_copy.wait()
    hidden_grad = jnp.dot(
        cot[...], down_full[...].reshape(-1, cols), preferred_element_type=jnp.float32
    )
    gate_grad = (
        hidden_grad * up_value * sigmoid_gate * (1.0 + gate_value * (1.0 - sigmoid_gate))
    ).astype(jnp.bfloat16)
    up_grad = (hidden_grad * gate_value * sigmoid_gate).astype(jnp.bfloat16)
    grads = jnp.concatenate([gate_grad, up_grad], axis=1)
    for copy in gate_copies + up_copies:
        copy.wait()
    for out, which in ((other_out, 1 - core), (mine_out, core)):
        for y in range(0, n_z, 2):
            pair = [
                jnp.concatenate([gate_full[y + i, which], up_full[y + i, which]], axis=1)
                for i in range(2)
            ]
            value = dot(grads, jnp.concatenate(pair), ((1,), (1,))).astype(jnp.bfloat16)
            out[y] = value[:, :wide]
            out[y + 1] = value[:, wide:]


def call_kernel(kernel, n_smem_any, operands, out_shapes, scratch, flops):
    in_specs = [pl.BlockSpec(memory_space=pltpu.SMEM)]
    in_specs += [pl.BlockSpec(memory_space=pl.ANY)] * n_smem_any
    in_specs += [pl.BlockSpec(memory_space=pltpu.VMEM)] * (len(operands) - 1 - n_smem_any)
    return pl.pallas_call(
        kernel,
        out_shape=out_shapes,
        in_specs=in_specs,
        out_specs=[pl.BlockSpec(memory_space=pltpu.VMEM)] * len(out_shapes),
        scratch_shapes=scratch,
        compiler_params=pltpu.CompilerParams(vmem_limit_bytes=60 * 1024 * 1024),
        cost_estimate=pl.CostEstimate(flops=flops, bytes_accessed=10_000_000, transcendentals=0),
    )(*operands)


def send_x(value, step):
    pairs = [
        (z * N_X + x, z * N_X + (x + step) % N_X) for z in range(N_Z) for x in range(N_X)
    ]
    return lax.ppermute(value, "fsdp", pairs)


def swap_z(value, flip):
    pairs = [(z * N_X + x, (z ^ flip) * N_X + x) for z in range(N_Z) for x in range(N_X)]
    return lax.ppermute(value, "fsdp", pairs)


def send_core(value):
    pairs = [(i, i ^ 1) for i in range(N_Y * N_CORE)]
    return lax.ppermute(value, "mp", pairs)


def copies_of(block):
    return jnp.broadcast_to(block[None], (N_Z,) + block.shape)


def gather_z(copies):
    return lax.all_to_all(copies, "fsdp", 0, 0, axis_index_groups=Z_GROUPS)


def add(left, right):
    return left.astype(jnp.float32) + right.astype(jnp.float32)


def on_device(tokens, cotangent, gate_weight, up_weight, down_weight):
    n_fsdp = lax.axis_size("fsdp")
    rows, width = tokens.shape
    depth, cols = gate_weight.shape
    n_feat = depth * n_fsdp
    factor = 1.0 / math.sqrt(rows * n_fsdp)
    me_x = lax.axis_index("fsdp") % N_X
    me_z = lax.axis_index("fsdp") // N_X
    core = lax.axis_index("mp") % N_CORE

    gate_copies = copies_of(gate_weight)
    gate_copies, tokens, cotangent = lax.optimization_barrier((gate_copies, tokens, cotangent))
    stacked = jnp.concatenate([tokens, cotangent])
    both = lax.all_gather(stacked, "mp", axis=1, tiled=True)

    down_x = jnp.zeros((N_X, depth, cols), down_weight.dtype)
    down_x = lax.dynamic_update_slice(down_x, down_weight[None], (me_x, 0, 0))
    for step in (1, N_X - 1, 2):
        block = send_x(down_weight, step)
        down_x = lax.dynamic_update_slice(down_x, block[None], ((me_x - step) % N_X, 0, 0))

    gate_z = gather_z(gate_copies)
    gate_left, gate_right = send_x(gate_z, 1), send_x(gate_z, -1)
    gate_z, up_copies = lax.optimization_barrier((gate_z, copies_of(up_weight)))
    up_z = gather_z(up_copies)
    up_z, down_copies, gate_left, gate_right = lax.optimization_barrier(
        (up_z, copies_of(down_x), gate_left, gate_right)
    )
    down_full = gather_z(down_copies).reshape(N_Z, N_CORE, 2 * depth, cols)

    up_right, up_left = send_x(up_z, -1), send_x(up_z, 1)
    gate_far, up_far = send_x(gate_left, 1), send_x(up_right, -1)
    blocks = (gate_z, gate_left, gate_right, gate_far, up_z, up_left, up_right, up_far)

    place = jnp.stack([me_x, core]).astype(jnp.int32)
    value = jax.ShapeDtypeStruct((rows, cols), jnp.float32)
    full = pltpu.VMEM((N_Z, N_CORE, 2 * depth, cols), jnp.bfloat16)
    row_block = pltpu.VMEM((rows, n_feat), jnp.bfloat16)
    sems = pltpu.SemaphoreType.DMA
    (gate_value,) = call_kernel(
        gate_kernel,
        5,
        (place, both) + blocks[:4],
        (value,),
        [row_block, full, sems((1,)), sems((N_X,))],
        2 * rows * n_feat * cols,
    )
    up_value, down_partial = call_kernel(
        forward_kernel,
        5,
        (place, both) + blocks[4:] + (gate_value,),
        (value, jax.ShapeDtypeStruct((N_X, N_Z, depth, cols), jnp.bfloat16)),
        [row_block, row_block, full, sems((2,)), sems((N_X,))],
        4 * rows * n_feat * cols,
    )
    half = jax.ShapeDtypeStruct((N_Y, rows, width), jnp.bfloat16)
    other, mine = call_kernel(
        backward_kernel,
        10,
        (place, both, down_full) + blocks + (gate_value, up_value),
        (half, half),
        [row_block, full, full, full, sems((1,)), sems((1,)), sems((N_X,)), sems((N_X,))],
        6 * rows * n_feat * cols,
    )
    pair_sum = add(mine, send_core(other)).astype(jnp.bfloat16)
    summed = lax.all_to_all(pair_sum, "mp", 0, 0, axis_index_groups=Y_GROUPS)

    down_x = lax.psum_scatter(
        down_partial.reshape(n_feat, cols),
        "fsdp",
        scatter_dimension=0,
        axis_index_groups=X_GROUPS,
        tiled=True,
    ).reshape(N_Z, depth, cols)
    block = lambda flip: lax.dynamic_index_in_dim(down_x, me_z ^ flip, 0, False)
    got = swap_z(jnp.stack([block(1 ^ flip) for flip in (0, 2, 6, 4)]), 1)
    mine_0, mine_2, mine_6, mine_4 = (add(block(f), got[i]) for i, f in enumerate((0, 2, 6, 4)))
    got = swap_z(jnp.stack([mine_2, mine_4]).astype(jnp.bfloat16), 2)
    got_last = swap_z((mine_6 + got[1].astype(jnp.float32)).astype(jnp.bfloat16), 6)
    down_sum = mine_0 + got[0].astype(jnp.float32) + got_last.astype(jnp.float32)
    grad_down = (down_sum * factor).astype(jnp.bfloat16)
    input_grad = summed.astype(jnp.float32).sum(0).astype(jnp.bfloat16)
    return (input_grad, grad_down)


def solution(mesh):
    placed = P("fsdp", "mp")
    return jax.shard_map(
        on_device,
        mesh=mesh,
        in_specs=(placed,) * 5,
        out_specs=(placed, placed),
        check_vma=False,
    )
```

```python
import math

import jax
import jax.numpy as jnp
from jax import lax
from jax.experimental import pallas as pl
from jax.experimental.pallas import tpu as pltpu
from jax.sharding import PartitionSpec as P

N_Z = 8
N_X = 4
N_Y = 8
N_CORE = 2
Z_GROUPS = [[z * N_X + x for z in range(N_Z)] for x in range(N_X)]
X_GROUPS = [[z * N_X + x for x in range(N_X)] for z in range(N_Z)]
Y_GROUPS = [[y * N_CORE + c for y in range(N_Y)] for c in range(N_CORE)]


def dot(left, right, dims):
    return lax.dot_general(left, right, (dims, ((), ())), preferred_element_type=jnp.float32)


def copy_blocks(blocks, full, sems, me_x, low=0, high=N_Z):
    depth = blocks[0].shape[1]
    part = pl.ds(low, high - low)
    copies = []
    for i, step in enumerate((0, N_X - 1, 1, 2)):
        x = lax.rem(me_x + step, N_X)
        row = pl.multiple_of(lax.rem(x, 2) * depth, depth)
        target = full.at[part, lax.div(x, 2), pl.ds(row, depth), :]
        copies.append(pltpu.make_async_copy(blocks[i].at[part], target, sems.at[i]))
    for copy in copies:
        copy.start()
    return copies


def gate_kernel(place, rows_ref, g0, g1, g2, g3, gate_out, tok, gate_full, row_sem, gate_sems):
    count, n_feat = tok.shape
    tok_copy = pltpu.make_async_copy(rows_ref.at[pl.ds(0, count)], tok, row_sem.at[0])
    tok_copy.start()
    gate_copies = copy_blocks((g0, g1, g2, g3), gate_full, gate_sems, place[0])
    tok_copy.wait()
    for copy in gate_copies:
        copy.wait()
    gate_out[...] = jnp.dot(
        tok[...], gate_full[...].reshape(n_feat, -1), preferred_element_type=jnp.float32
    )


def forward_kernel(
    place, rows_ref, u0, u1, u2, u3, gate_in, up_out, partial_out,
    tok, cot, up_full, partial_full, row_sems, low_sems, high_sems, out_sems,
):
    count, n_feat = tok.shape
    half = n_feat // 2
    halves = (pl.ds(0, half), pl.ds(half, half))
    blocks = (u0, u1, u2, u3)
    rows = [
        pltpu.make_async_copy(
            rows_ref.at[pl.ds(0, count), part], tok.at[:, part], row_sems.at[i]
        )
        for i, part in enumerate(halves)
    ]
    cot_copy = pltpu.make_async_copy(rows_ref.at[pl.ds(count, count)], cot, row_sems.at[2])
    rows[0].start()
    low_copies = copy_blocks(blocks, up_full, low_sems, place[0], 0, N_Z // 2)
    rows[1].start()
    high_copies = copy_blocks(blocks, up_full, high_sems, place[0], N_Z // 2, N_Z)
    cot_copy.start()
    gate_value = gate_in[...]
    silu = gate_value * jax.nn.sigmoid(gate_value)
    for copy in [rows[0]] + low_copies:
        copy.wait()
    up_value = jnp.dot(
        tok[:, :half], up_full[: N_Z // 2].reshape(half, -1), preferred_element_type=jnp.float32
    )
    for copy in [rows[1]] + high_copies:
        copy.wait()
    up_value = up_value + jnp.dot(
        tok[:, half:], up_full[N_Z // 2 :].reshape(half, -1), preferred_element_type=jnp.float32
    )
    up_out[...] = up_value
    hidden = (silu * up_value).astype(jnp.bfloat16)
    cot_copy.wait()
    depth = n_feat // (N_Z * N_X)
    outs = []
    for i in range(2):
        value = dot(cot[:, i * half : (i + 1) * half], hidden, ((0,), (0,))).astype(jnp.bfloat16)
        for z in range(N_Z // 2):
            for x in range(N_X):
                row = (z * N_X + x) * depth
                partial_full[x, i * (N_Z // 2) + z] = value[row : row + depth]
        part = pl.ds(i * (N_Z // 2), N_Z // 2)
        outs.append(
            pltpu.make_async_copy(partial_full.at[:, part], partial_out.at[:, part], out_sems.at[i])
        )
        outs[i].start()
    for copy in outs:
        copy.wait()


def backward_kernel(
    place, rows_ref, down_ref, g0, g1, g2, g3, u0, u1, u2, u3, gate_in, up_in, other_out, mine_out,
    cot, down_full, gate_full, up_full, row_sems, down_sems, gate_sems, up_sems,
):
    me_x, core = place[0], place[1]
    count, n_feat = cot.shape
    n_z, _, wide, cols = gate_full.shape
    half, half_z = n_feat // 2, n_z // 2
    first = []
    for i in range(2):
        columns, part = pl.ds(i * half, half), pl.ds(i * half_z, half_z)
        first.append(
            (
                pltpu.make_async_copy(
                    rows_ref.at[pl.ds(count, count), columns], cot.at[:, columns], row_sems.at[i]
                ),
                pltpu.make_async_copy(down_ref.at[part], down_full.at[part], down_sems.at[i]),
            )
        )
    for pair in first:
        for copy in pair:
            copy.start()
    gate_copies = copy_blocks((g0, g1, g2, g3), gate_full, gate_sems, me_x)
    up_copies = copy_blocks((u0, u1, u2, u3), up_full, up_sems, me_x)
    gate_value, up_value = gate_in[...], up_in[...]
    sigmoid_gate = jax.nn.sigmoid(gate_value)
    up_factor = gate_value * sigmoid_gate
    gate_factor = up_value * sigmoid_gate * (1.0 + gate_value * (1.0 - sigmoid_gate))
    for copy in first[0]:
        copy.wait()
    hidden_grad = jnp.dot(
        cot[:, :half], down_full[:half_z].reshape(half, cols), preferred_element_type=jnp.float32
    )
    for copy in first[1]:
        copy.wait()
    hidden_grad = hidden_grad + jnp.dot(
        cot[:, half:], down_full[half_z:].reshape(half, cols), preferred_element_type=jnp.float32
    )
    gate_grad = (hidden_grad * gate_factor).astype(jnp.bfloat16)
    up_grad = (hidden_grad * up_factor).astype(jnp.bfloat16)
    grads = jnp.concatenate([gate_grad, up_grad], axis=1)
    for copy in gate_copies + up_copies:
        copy.wait()
    for out, which in ((other_out, 1 - core), (mine_out, core)):
        for y in range(0, n_z, 2):
            pair = [
                jnp.concatenate([gate_full[y + i, which], up_full[y + i, which]], axis=1)
                for i in range(2)
            ]
            value = dot(grads, jnp.concatenate(pair), ((1,), (1,))).astype(jnp.bfloat16)
            out[y] = value[:, :wide]
            out[y + 1] = value[:, wide:]


def call_kernel(kernel, n_smem_any, operands, out_shapes, scratch, flops, out_any=()):
    in_specs = [pl.BlockSpec(memory_space=pltpu.SMEM)]
    in_specs += [pl.BlockSpec(memory_space=pl.ANY)] * n_smem_any
    in_specs += [pl.BlockSpec(memory_space=pltpu.VMEM)] * (len(operands) - 1 - n_smem_any)
    return pl.pallas_call(
        kernel,
        out_shape=out_shapes,
        in_specs=in_specs,
        out_specs=[
            pl.BlockSpec(memory_space=pl.ANY if i in out_any else pltpu.VMEM)
            for i in range(len(out_shapes))
        ],
        scratch_shapes=scratch,
        compiler_params=pltpu.CompilerParams(vmem_limit_bytes=60 * 1024 * 1024),
        cost_estimate=pl.CostEstimate(flops=flops, bytes_accessed=10_000_000, transcendentals=0),
    )(*operands)


def send_x(value, step):
    pairs = [
        (z * N_X + x, z * N_X + (x + step) % N_X) for z in range(N_Z) for x in range(N_X)
    ]
    return lax.ppermute(value, "fsdp", pairs)


def swap_z(value, flip):
    pairs = [(z * N_X + x, (z ^ flip) * N_X + x) for z in range(N_Z) for x in range(N_X)]
    return lax.ppermute(value, "fsdp", pairs)


def send_core(value):
    pairs = [(i, i ^ 1) for i in range(N_Y * N_CORE)]
    return lax.ppermute(value, "mp", pairs)


def copies_of(block):
    return jnp.broadcast_to(block[None], (N_Z,) + block.shape)


def gather_z(copies):
    return lax.all_to_all(copies, "fsdp", 0, 0, axis_index_groups=Z_GROUPS)


def add(left, right):
    return left.astype(jnp.float32) + right.astype(jnp.float32)


def on_device(tokens, cotangent, gate_weight, up_weight, down_weight):
    n_fsdp = lax.axis_size("fsdp")
    rows, width = tokens.shape
    depth, cols = gate_weight.shape
    n_feat = depth * n_fsdp
    factor = 1.0 / math.sqrt(rows * n_fsdp)
    me_x = lax.axis_index("fsdp") % N_X
    me_z = lax.axis_index("fsdp") // N_X
    core = lax.axis_index("mp") % N_CORE

    down_blocks = [send_x(down_weight, step) for step in (1, N_X - 1, 2)]
    down_x = jnp.zeros((N_X, depth, cols), down_weight.dtype)
    down_x = lax.dynamic_update_slice(down_x, down_weight[None], (me_x, 0, 0))
    for step, block in zip((1, N_X - 1, 2), down_blocks):
        down_x = lax.dynamic_update_slice(down_x, block[None], ((me_x - step) % N_X, 0, 0))

    first, tokens, cotangent = lax.optimization_barrier((down_blocks[0], tokens, cotangent))
    stacked = jnp.concatenate([tokens, cotangent])
    both = lax.all_gather(stacked, "mp", axis=1, tiled=True)

    gate_z = gather_z(copies_of(gate_weight))
    gate_z, up_copies, down_copies = lax.optimization_barrier(
        (gate_z, copies_of(up_weight), copies_of(down_x))
    )
    gate_left, gate_right = send_x(gate_z, 1), send_x(gate_z, -1)
    up_z = gather_z(up_copies)
    up_z, down_copies, gate_left, gate_right = lax.optimization_barrier(
        (up_z, down_copies, gate_left, gate_right)
    )
    down_full = gather_z(down_copies).reshape(N_Z, N_CORE, 2 * depth, cols)

    up_right, up_left = send_x(up_z, -1), send_x(up_z, 1)
    gate_far, up_far = send_x(gate_left, 1), send_x(up_right, -1)
    blocks = (gate_z, gate_left, gate_right, gate_far, up_z, up_left, up_right, up_far)

    place = jnp.stack([me_x, core]).astype(jnp.int32)
    value = jax.ShapeDtypeStruct((rows, cols), jnp.float32)
    full = pltpu.VMEM((N_Z, N_CORE, 2 * depth, cols), jnp.bfloat16)
    row_block = pltpu.VMEM((rows, n_feat), jnp.bfloat16)
    sems = pltpu.SemaphoreType.DMA
    (gate_value,) = call_kernel(
        gate_kernel,
        5,
        (place, both) + blocks[:4],
        (value,),
        [row_block, full, sems((1,)), sems((N_X,))],
        2 * rows * n_feat * cols,
    )
    up_value, down_partial = call_kernel(
        forward_kernel,
        5,
        (place, both) + blocks[4:] + (gate_value,),
        (value, jax.ShapeDtypeStruct((N_X, N_Z, depth, cols), jnp.bfloat16)),
        [row_block, row_block, full, pltpu.VMEM((N_X, N_Z, depth, cols), jnp.bfloat16)]
        + [sems((3,)), sems((N_X,)), sems((N_X,)), sems((2,))],
        4 * rows * n_feat * cols,
        (1,),
    )
    half = jax.ShapeDtypeStruct((N_Y, rows, width), jnp.bfloat16)
    other, mine = call_kernel(
        backward_kernel,
        10,
        (place, both, down_full) + blocks + (gate_value, up_value),
        (half, half),
        [row_block, full, full, full, sems((2,)), sems((2,)), sems((N_X,)), sems((N_X,))],
        6 * rows * n_feat * cols,
    )
    pair_sum = add(mine, send_core(other)).astype(jnp.bfloat16)
    summed = lax.all_to_all(pair_sum, "mp", 0, 0, axis_index_groups=Y_GROUPS)

    down_x = lax.psum_scatter(
        down_partial.reshape(n_feat, cols),
        "fsdp",
        scatter_dimension=0,
        axis_index_groups=X_GROUPS,
        tiled=True,
    ).reshape(N_Z, depth, cols)
    block = lambda flip: lax.dynamic_index_in_dim(down_x, me_z ^ flip, 0, False)
    got = swap_z(jnp.stack([block(1 ^ flip) for flip in (0, 2, 6, 4)]), 1)
    mine_0, mine_2, mine_6, mine_4 = (add(block(f), got[i]) for i, f in enumerate((0, 2, 6, 4)))
    got = swap_z(jnp.stack([mine_2, mine_4]).astype(jnp.bfloat16), 2)
    got_last = swap_z((mine_6 + got[1].astype(jnp.float32)).astype(jnp.bfloat16), 6)
    down_sum = mine_0 + got[0].astype(jnp.float32) + got_last.astype(jnp.float32)
    grad_down = (down_sum * factor).astype(jnp.bfloat16)
    input_grad = summed.astype(jnp.float32).sum(0).astype(jnp.bfloat16)
    return (input_grad, grad_down)


def solution(mesh):
    placed = P("fsdp", "mp")
    return jax.shard_map(
        on_device,
        mesh=mesh,
        in_specs=(placed,) * 5,
        out_specs=(placed, placed),
        check_vma=False,
    )
```

```python
import math

import jax
import jax.numpy as jnp
from jax import lax
from jax.experimental import pallas as pl
from jax.experimental.pallas import tpu as pltpu
from jax.sharding import PartitionSpec as P

N_Z = 8
N_X = 4
N_Y = 8
N_CORE = 2
Z_GROUPS = [[z * N_X + x for z in range(N_Z)] for x in range(N_X)]
X_GROUPS = [[z * N_X + x for x in range(N_X)] for z in range(N_Z)]
Y_GROUPS = [[y * N_CORE + c for y in range(N_Y)] for c in range(N_CORE)]


def dot(left, right, dims):
    return lax.dot_general(left, right, (dims, ((), ())), preferred_element_type=jnp.float32)


def copy_blocks(blocks, full, sems, me_x):
    depth = blocks[0].shape[1]
    copies = []
    for i, step in enumerate((0, N_X - 1, 1, 2)):
        x = lax.rem(me_x + step, N_X)
        row = pl.multiple_of(lax.rem(x, 2) * depth, depth)
        target = full.at[:, lax.div(x, 2), pl.ds(row, depth), :]
        copies.append(pltpu.make_async_copy(blocks[i], target, sems.at[i]))
    for copy in copies:
        copy.start()
    return copies


def forward_kernel(
    place, rows_ref, g0, g1, g2, g3, u0, u1, u2, u3, gate_out, up_out, partial_out,
    tok, cot, gate_full, up_full, row_sems, gate_sems, up_sems,
):
    count, n_feat = tok.shape
    tok_copy = pltpu.make_async_copy(rows_ref.at[pl.ds(0, count)], tok, row_sems.at[0])
    cot_copy = pltpu.make_async_copy(rows_ref.at[pl.ds(count, count)], cot, row_sems.at[1])
    tok_copy.start()
    gate_copies = copy_blocks((g0, g1, g2, g3), gate_full, gate_sems, place[0])
    up_copies = copy_blocks((u0, u1, u2, u3), up_full, up_sems, place[0])
    cot_copy.start()
    tok_copy.wait()
    for copy in gate_copies:
        copy.wait()
    gate_value = jnp.dot(
        tok[...], gate_full[...].reshape(n_feat, -1), preferred_element_type=jnp.float32
    )
    gate_out[...] = gate_value
    for copy in up_copies:
        copy.wait()
    up_value = jnp.dot(
        tok[...], up_full[...].reshape(n_feat, -1), preferred_element_type=jnp.float32
    )
    up_out[...] = up_value
    hidden = (gate_value * jax.nn.sigmoid(gate_value) * up_value).astype(jnp.bfloat16)
    cot_copy.wait()
    partial_value = dot(cot[...], hidden, ((0,), (0,))).astype(jnp.bfloat16)
    depth = n_feat // (N_Z * N_X)
    for z in range(N_Z):
        for x in range(N_X):
            row = (z * N_X + x) * depth
            partial_out[x, z] = partial_value[row : row + depth]


def backward_kernel(
    place, rows_ref, down_ref, g0, g1, g2, g3, u0, u1, u2, u3, gate_in, up_in, other_out, mine_out,
    cot, down_full, gate_full, up_full, row_sem, down_sem, gate_sems, up_sems,
):
    me_x, core = place[0], place[1]
    count = cot.shape[0]
    n_z, _, wide, cols = gate_full.shape
    cot_copy = pltpu.make_async_copy(rows_ref.at[pl.ds(count, count)], cot, row_sem.at[0])
    down_copy = pltpu.make_async_copy(down_ref, down_full, down_sem.at[0])
    cot_copy.start()
    down_copy.start()
    gate_copies = copy_blocks((g0, g1, g2, g3), gate_full, gate_sems, me_x)
    up_copies = copy_blocks((u0, u1, u2, u3), up_full, up_sems, me_x)
    gate_value, up_value = gate_in[...], up_in[...]
    sigmoid_gate = jax.nn.sigmoid(gate_value)
    cot_copy.wait()
    down_copy.wait()
    hidden_grad = jnp.dot(
        cot[...], down_full[...].reshape(-1, cols), preferred_element_type=jnp.float32
    )
    gate_grad = (
        hidden_grad * up_value * sigmoid_gate * (1.0 + gate_value * (1.0 - sigmoid_gate))
    ).astype(jnp.bfloat16)
    up_grad = (hidden_grad * gate_value * sigmoid_gate).astype(jnp.bfloat16)
    grads = jnp.concatenate([gate_grad, up_grad], axis=1)
    for copy in gate_copies + up_copies:
        copy.wait()
    for out, which in ((other_out, 1 - core), (mine_out, core)):
        for y in range(0, n_z, 2):
            pair = [
                jnp.concatenate([gate_full[y + i, which], up_full[y + i, which]], axis=1)
                for i in range(2)
            ]
            value = dot(grads, jnp.concatenate(pair), ((1,), (1,))).astype(jnp.bfloat16)
            out[y] = value[:, :wide]
            out[y + 1] = value[:, wide:]


def call_kernel(kernel, n_smem_any, operands, out_shapes, scratch, flops):
    in_specs = [pl.BlockSpec(memory_space=pltpu.SMEM)]
    in_specs += [pl.BlockSpec(memory_space=pl.ANY)] * n_smem_any
    in_specs += [pl.BlockSpec(memory_space=pltpu.VMEM)] * (len(operands) - 1 - n_smem_any)
    return pl.pallas_call(
        kernel,
        out_shape=out_shapes,
        in_specs=in_specs,
        out_specs=[pl.BlockSpec(memory_space=pltpu.VMEM)] * len(out_shapes),
        scratch_shapes=scratch,
        compiler_params=pltpu.CompilerParams(vmem_limit_bytes=60 * 1024 * 1024),
        cost_estimate=pl.CostEstimate(flops=flops, bytes_accessed=10_000_000, transcendentals=0),
    )(*operands)


def send_x(value, step):
    pairs = [
        (z * N_X + x, z * N_X + (x + step) % N_X) for z in range(N_Z) for x in range(N_X)
    ]
    return lax.ppermute(value, "fsdp", pairs)


def swap_z(value, flip):
    pairs = [(z * N_X + x, (z ^ flip) * N_X + x) for z in range(N_Z) for x in range(N_X)]
    return lax.ppermute(value, "fsdp", pairs)


def send_core(value):
    pairs = [(i, i ^ 1) for i in range(N_Y * N_CORE)]
    return lax.ppermute(value, "mp", pairs)


def copies_of(block):
    return jnp.broadcast_to(block[None], (N_Z,) + block.shape)


def gather_z(copies):
    return lax.all_to_all(copies, "fsdp", 0, 0, axis_index_groups=Z_GROUPS)


def add(left, right):
    return left.astype(jnp.float32) + right.astype(jnp.float32)


def on_device(tokens, cotangent, gate_weight, up_weight, down_weight):
    n_fsdp = lax.axis_size("fsdp")
    rows, width = tokens.shape
    depth, cols = gate_weight.shape
    n_feat = depth * n_fsdp
    factor = 1.0 / math.sqrt(rows * n_fsdp)
    me_x = lax.axis_index("fsdp") % N_X
    me_z = lax.axis_index("fsdp") // N_X
    core = lax.axis_index("mp") % N_CORE

    gate_copies = copies_of(gate_weight)
    gate_copies, tokens, cotangent = lax.optimization_barrier((gate_copies, tokens, cotangent))
    stacked = jnp.concatenate([tokens, cotangent])
    both = lax.all_gather(stacked, "mp", axis=1, tiled=True)

    down_x = jnp.zeros((N_X, depth, cols), down_weight.dtype)
    down_x = lax.dynamic_update_slice(down_x, down_weight[None], (me_x, 0, 0))
    for step in (1, N_X - 1, 2):
        block = send_x(down_weight, step)
        down_x = lax.dynamic_update_slice(down_x, block[None], ((me_x - step) % N_X, 0, 0))

    gate_z = gather_z(gate_copies)
    gate_left, gate_right = send_x(gate_z, 1), send_x(gate_z, -1)
    gate_z, up_copies = lax.optimization_barrier((gate_z, copies_of(up_weight)))
    up_z = gather_z(up_copies)
    up_z, down_copies, gate_left, gate_right = lax.optimization_barrier(
        (up_z, copies_of(down_x), gate_left, gate_right)
    )
    down_full = gather_z(down_copies).reshape(N_Z, N_CORE, 2 * depth, cols)

    up_right, up_left = send_x(up_z, -1), send_x(up_z, 1)
    gate_far, up_far = send_x(gate_left, 1), send_x(up_right, -1)
    blocks = (gate_z, gate_left, gate_right, gate_far, up_z, up_left, up_right, up_far)

    place = jnp.stack([me_x, core]).astype(jnp.int32)
    value = jax.ShapeDtypeStruct((rows, cols), jnp.float32)
    full = pltpu.VMEM((N_Z, N_CORE, 2 * depth, cols), jnp.bfloat16)
    row_block = pltpu.VMEM((rows, n_feat), jnp.bfloat16)
    sems = pltpu.SemaphoreType.DMA
    gate_value, up_value, down_partial = call_kernel(
        forward_kernel,
        9,
        (place, both) + blocks,
        (value, value, jax.ShapeDtypeStruct((N_X, N_Z, depth, cols), jnp.bfloat16)),
        [row_block, row_block, full, full, sems((2,)), sems((N_X,)), sems((N_X,))],
        6 * rows * n_feat * cols,
    )
    half = jax.ShapeDtypeStruct((N_Y, rows, width), jnp.bfloat16)
    other, mine = call_kernel(
        backward_kernel,
        10,
        (place, both, down_full) + blocks + (gate_value, up_value),
        (half, half),
        [row_block, full, full, full, sems((1,)), sems((1,)), sems((N_X,)), sems((N_X,))],
        6 * rows * n_feat * cols,
    )
    pair_sum = add(mine, send_core(other)).astype(jnp.bfloat16)
    summed = lax.all_to_all(pair_sum, "mp", 0, 0, axis_index_groups=Y_GROUPS)

    down_x = lax.psum_scatter(
        down_partial.reshape(n_feat, cols),
        "fsdp",
        scatter_dimension=0,
        axis_index_groups=X_GROUPS,
        tiled=True,
    ).reshape(N_Z, depth, cols)
    block = lambda flip: lax.dynamic_index_in_dim(down_x, me_z ^ flip, 0, False)
    got = swap_z(jnp.stack([block(1 ^ flip) for flip in (0, 2, 6, 4)]), 1)
    mine_0, mine_2, mine_6, mine_4 = (add(block(f), got[i]) for i, f in enumerate((0, 2, 6, 4)))
    got = swap_z(jnp.stack([mine_2, mine_4]).astype(jnp.bfloat16), 2)
    got_last = swap_z((mine_6 + got[1].astype(jnp.float32)).astype(jnp.bfloat16), 6)
    down_sum = mine_0 + got[0].astype(jnp.float32) + got_last.astype(jnp.float32)
    grad_down = (down_sum * factor).astype(jnp.bfloat16)
    input_grad = summed.astype(jnp.float32).sum(0).astype(jnp.bfloat16)
    return (input_grad, grad_down)


def solution(mesh):
    placed = P("fsdp", "mp")
    return jax.shard_map(
        on_device,
        mesh=mesh,
        in_specs=(placed,) * 5,
        out_specs=(placed, placed),
        check_vma=False,
    )
```

```python
import math

import jax
import jax.numpy as jnp
from jax import lax
from jax.experimental import pallas as pl
from jax.experimental.pallas import tpu as pltpu
from jax.sharding import PartitionSpec as P

N_Z = 8
N_X = 4
N_Y = 8
N_CORE = 2
Z_GROUPS = [[z * N_X + x for z in range(N_Z)] for x in range(N_X)]
PAIR_GROUPS = [
    [z * N_X + x for x in range(N_X)] + [(z + 1) * N_X + x for x in reversed(range(N_X))]
    for z in range(0, N_Z, 2)
]
Y_GROUPS = [[y * N_CORE + c for y in range(N_Y)] for c in range(N_CORE)]


def dot(left, right, dims):
    return lax.dot_general(left, right, (dims, ((), ())), preferred_element_type=jnp.float32)


def pair_place(odd, x):
    return 2 * N_X - 1 - x if odd else x


def copy_blocks(blocks, full, sems, me_x):
    depth = blocks[0].shape[1]
    copies = []
    for i, step in enumerate((0, N_X - 1, 1, 2)):
        x = lax.rem(me_x + step, N_X)
        row = pl.multiple_of(lax.rem(x, 2) * depth, depth)
        target = full.at[:, lax.div(x, 2), pl.ds(row, depth), :]
        copies.append(pltpu.make_async_copy(blocks[i], target, sems.at[i]))
    for copy in copies:
        copy.start()
    return copies


def forward_kernel(
    place, rows_ref, g0, g1, g2, g3, u0, u1, u2, u3, gate_out, up_out, partial_out,
    tok, cot, gate_full, up_full, row_sems, gate_sems, up_sems,
):
    count, n_feat = tok.shape
    tok_copy = pltpu.make_async_copy(rows_ref.at[pl.ds(0, count)], tok, row_sems.at[0])
    cot_copy = pltpu.make_async_copy(rows_ref.at[pl.ds(count, count)], cot, row_sems.at[1])
    tok_copy.start()
    gate_copies = copy_blocks((g0, g1, g2, g3), gate_full, gate_sems, place[0])
    up_copies = copy_blocks((u0, u1, u2, u3), up_full, up_sems, place[0])
    cot_copy.start()
    tok_copy.wait()
    for copy in gate_copies:
        copy.wait()
    gate_value = jnp.dot(
        tok[...], gate_full[...].reshape(n_feat, -1), preferred_element_type=jnp.float32
    )
    gate_out[...] = gate_value
    for copy in up_copies:
        copy.wait()
    up_value = jnp.dot(
        tok[...], up_full[...].reshape(n_feat, -1), preferred_element_type=jnp.float32
    )
    up_out[...] = up_value
    hidden = (gate_value * jax.nn.sigmoid(gate_value) * up_value).astype(jnp.bfloat16)
    cot_copy.wait()
    partial_value = dot(cot[...], hidden, ((0,), (0,))).astype(jnp.bfloat16)
    depth = n_feat // (N_Z * N_X)
    for z in range(N_Z):
        for x in range(N_X):
            row = (z * N_X + x) * depth
            partial_out[pair_place(z % 2, x), z // 2] = partial_value[row : row + depth]


def backward_kernel(
    place, rows_ref, down_ref, g0, g1, g2, g3, u0, u1, u2, u3, gate_in, up_in, other_out, mine_out,
    cot, down_full, gate_full, up_full, row_sem, down_sem, gate_sems, up_sems,
):
    me_x, core = place[0], place[1]
    count = cot.shape[0]
    n_z, _, wide, cols = gate_full.shape
    cot_copy = pltpu.make_async_copy(rows_ref.at[pl.ds(count, count)], cot, row_sem.at[0])
    down_copy = pltpu.make_async_copy(down_ref, down_full, down_sem.at[0])
    cot_copy.start()
    down_copy.start()
    gate_copies = copy_blocks((g0, g1, g2, g3), gate_full, gate_sems, me_x)
    up_copies = copy_blocks((u0, u1, u2, u3), up_full, up_sems, me_x)
    gate_value, up_value = gate_in[...], up_in[...]
    sigmoid_gate = jax.nn.sigmoid(gate_value)
    cot_copy.wait()
    down_copy.wait()
    hidden_grad = jnp.dot(
        cot[...], down_full[...].reshape(-1, cols), preferred_element_type=jnp.float32
    )
    gate_grad = (
        hidden_grad * up_value * sigmoid_gate * (1.0 + gate_value * (1.0 - sigmoid_gate))
    ).astype(jnp.bfloat16)
    up_grad = (hidden_grad * gate_value * sigmoid_gate).astype(jnp.bfloat16)
    grads = jnp.concatenate([gate_grad, up_grad], axis=1)
    for copy in gate_copies + up_copies:
        copy.wait()
    for out, which in ((other_out, 1 - core), (mine_out, core)):
        for y in range(0, n_z, 2):
            pair = [
                jnp.concatenate([gate_full[y + i, which], up_full[y + i, which]], axis=1)
                for i in range(2)
            ]
            value = dot(grads, jnp.concatenate(pair), ((1,), (1,))).astype(jnp.bfloat16)
            out[y] = value[:, :wide]
            out[y + 1] = value[:, wide:]


def call_kernel(kernel, n_smem_any, operands, out_shapes, scratch, flops):
    in_specs = [pl.BlockSpec(memory_space=pltpu.SMEM)]
    in_specs += [pl.BlockSpec(memory_space=pl.ANY)] * n_smem_any
    in_specs += [pl.BlockSpec(memory_space=pltpu.VMEM)] * (len(operands) - 1 - n_smem_any)
    return pl.pallas_call(
        kernel,
        out_shape=out_shapes,
        in_specs=in_specs,
        out_specs=[pl.BlockSpec(memory_space=pltpu.VMEM)] * len(out_shapes),
        scratch_shapes=scratch,
        compiler_params=pltpu.CompilerParams(vmem_limit_bytes=60 * 1024 * 1024),
        cost_estimate=pl.CostEstimate(flops=flops, bytes_accessed=10_000_000, transcendentals=0),
    )(*operands)


def send_x(value, step):
    pairs = [
        (z * N_X + x, z * N_X + (x + step) % N_X) for z in range(N_Z) for x in range(N_X)
    ]
    return lax.ppermute(value, "fsdp", pairs)


def swap_z(value, flip):
    pairs = [(z * N_X + x, (z ^ flip) * N_X + x) for z in range(N_Z) for x in range(N_X)]
    return lax.ppermute(value, "fsdp", pairs)


def send_core(value):
    pairs = [(i, i ^ 1) for i in range(N_Y * N_CORE)]
    return lax.ppermute(value, "mp", pairs)


def copies_of(block):
    return jnp.broadcast_to(block[None], (N_Z,) + block.shape)


def gather_z(copies):
    return lax.all_to_all(copies, "fsdp", 0, 0, axis_index_groups=Z_GROUPS)


def add(left, right):
    return left.astype(jnp.float32) + right.astype(jnp.float32)


def on_device(tokens, cotangent, gate_weight, up_weight, down_weight):
    n_fsdp = lax.axis_size("fsdp")
    rows, width = tokens.shape
    depth, cols = gate_weight.shape
    n_feat = depth * n_fsdp
    factor = 1.0 / math.sqrt(rows * n_fsdp)
    me_x = lax.axis_index("fsdp") % N_X
    me_z = lax.axis_index("fsdp") // N_X
    core = lax.axis_index("mp") % N_CORE

    gate_copies = copies_of(gate_weight)
    gate_copies, tokens, cotangent = lax.optimization_barrier((gate_copies, tokens, cotangent))
    stacked = jnp.concatenate([tokens, cotangent])
    both = lax.all_gather(stacked, "mp", axis=1, tiled=True)

    down_x = jnp.zeros((N_X, depth, cols), down_weight.dtype)
    down_x = lax.dynamic_update_slice(down_x, down_weight[None], (me_x, 0, 0))
    for step in (1, N_X - 1, 2):
        block = send_x(down_weight, step)
        down_x = lax.dynamic_update_slice(down_x, block[None], ((me_x - step) % N_X, 0, 0))

    gate_z = gather_z(gate_copies)
    gate_left, gate_right = send_x(gate_z, 1), send_x(gate_z, -1)
    gate_z, up_copies = lax.optimization_barrier((gate_z, copies_of(up_weight)))
    up_z = gather_z(up_copies)
    up_z, down_copies, gate_left, gate_right = lax.optimization_barrier(
        (up_z, copies_of(down_x), gate_left, gate_right)
    )
    down_full = gather_z(down_copies).reshape(N_Z, N_CORE, 2 * depth, cols)

    up_right, up_left = send_x(up_z, -1), send_x(up_z, 1)
    gate_far, up_far = send_x(gate_left, 1), send_x(up_right, -1)
    blocks = (gate_z, gate_left, gate_right, gate_far, up_z, up_left, up_right, up_far)

    place = jnp.stack([me_x, core]).astype(jnp.int32)
    value = jax.ShapeDtypeStruct((rows, cols), jnp.float32)
    full = pltpu.VMEM((N_Z, N_CORE, 2 * depth, cols), jnp.bfloat16)
    row_block = pltpu.VMEM((rows, n_feat), jnp.bfloat16)
    sems = pltpu.SemaphoreType.DMA
    gate_value, up_value, down_partial = call_kernel(
        forward_kernel,
        9,
        (place, both) + blocks,
        (value, value, jax.ShapeDtypeStruct((2 * N_X, N_Z // 2, depth, cols), jnp.bfloat16)),
        [row_block, row_block, full, full, sems((2,)), sems((N_X,)), sems((N_X,))],
        6 * rows * n_feat * cols,
    )
    half = jax.ShapeDtypeStruct((N_Y, rows, width), jnp.bfloat16)
    other, mine = call_kernel(
        backward_kernel,
        10,
        (place, both, down_full) + blocks + (gate_value, up_value),
        (half, half),
        [row_block, full, full, full, sems((1,)), sems((1,)), sems((N_X,)), sems((N_X,))],
        6 * rows * n_feat * cols,
    )
    pair_sum = add(mine, send_core(other)).astype(jnp.bfloat16)
    summed = lax.all_to_all(pair_sum, "mp", 0, 0, axis_index_groups=Y_GROUPS)

    down_pair = lax.psum_scatter(
        down_partial.reshape(n_feat, cols),
        "fsdp",
        scatter_dimension=0,
        axis_index_groups=PAIR_GROUPS,
        tiled=True,
    ).reshape(N_Z // 2, depth, cols)
    block = lambda flip: lax.dynamic_index_in_dim(down_pair, (me_z // 2) ^ (flip // 2), 0, False)
    got = swap_z(jnp.stack([block(2), block(4)]), 2)
    got_last = swap_z(add(block(6), got[1]).astype(jnp.bfloat16), 6)
    down_sum = add(block(0), got[0]) + got_last.astype(jnp.float32)
    grad_down = (down_sum * factor).astype(jnp.bfloat16)
    input_grad = summed.astype(jnp.float32).sum(0).astype(jnp.bfloat16)
    return (input_grad, grad_down)


def solution(mesh):
    placed = P("fsdp", "mp")
    return jax.shard_map(
        on_device,
        mesh=mesh,
        in_specs=(placed,) * 5,
        out_specs=(placed, placed),
        check_vma=False,
    )
```

```python
import math

import jax
import jax.numpy as jnp
from jax import lax
from jax.experimental import pallas as pl
from jax.experimental.pallas import tpu as pltpu
from jax.sharding import PartitionSpec as P

N_Z = 8
N_X = 4
N_Y = 8
N_CORE = 2
Z_GROUPS = [[z * N_X + x for z in range(N_Z)] for x in range(N_X)]
PAIR_GROUPS = [
    [z * N_X + x for x in range(N_X)] + [(z + 1) * N_X + x for x in reversed(range(N_X))]
    for z in range(0, N_Z, 2)
]
Y_GROUPS = [[y * N_CORE + c for y in range(N_Y)] for c in range(N_CORE)]


def dot(left, right, dims):
    return lax.dot_general(left, right, (dims, ((), ())), preferred_element_type=jnp.float32)


def pair_place(odd, x):
    return 2 * N_X - 1 - x if odd else x


def copy_blocks(blocks, full, sems, me_x):
    depth = blocks[0].shape[1]
    copies = []
    for i, step in enumerate((0, N_X - 1, 1, 2)):
        x = lax.rem(me_x + step, N_X)
        row = pl.multiple_of(lax.rem(x, 2) * depth, depth)
        target = full.at[:, lax.div(x, 2), pl.ds(row, depth), :]
        copies.append(pltpu.make_async_copy(blocks[i], target, sems.at[i]))
    for copy in copies:
        copy.start()
    return copies


def forward_kernel(
    place, rows_ref, g0, g1, g2, g3, u0, u1, u2, u3, gate_out, up_out, partial_out,
    tok, cot, gate_full, up_full, row_sems, gate_sems, up_sems,
):
    count, n_feat = tok.shape
    tok_copy = pltpu.make_async_copy(rows_ref.at[pl.ds(0, count)], tok, row_sems.at[0])
    cot_copy = pltpu.make_async_copy(rows_ref.at[pl.ds(count, count)], cot, row_sems.at[1])
    tok_copy.start()
    gate_copies = copy_blocks((g0, g1, g2, g3), gate_full, gate_sems, place[0])
    up_copies = copy_blocks((u0, u1, u2, u3), up_full, up_sems, place[0])
    cot_copy.start()
    tok_copy.wait()
    for copy in gate_copies:
        copy.wait()
    gate_value = jnp.dot(
        tok[...], gate_full[...].reshape(n_feat, -1), preferred_element_type=jnp.float32
    )
    gate_out[...] = gate_value
    for copy in up_copies:
        copy.wait()
    up_value = jnp.dot(
        tok[...], up_full[...].reshape(n_feat, -1), preferred_element_type=jnp.float32
    )
    up_out[...] = up_value
    hidden = (gate_value * sigmoid(gate_value) * up_value).astype(jnp.bfloat16)
    cot_copy.wait()
    partial_value = dot(cot[...], hidden, ((0,), (0,))).astype(jnp.bfloat16)
    depth = n_feat // (N_Z * N_X)
    for z in range(N_Z):
        for x in range(N_X):
            row = (z * N_X + x) * depth
            partial_out[pair_place(z % 2, x), z // 2] = partial_value[row : row + depth]


def backward_kernel(
    place, rows_ref, down_ref, g0, g1, g2, g3, u0, u1, u2, u3, gate_in, up_in, other_out, mine_out,
    cot, down_full, gate_full, up_full, row_sem, down_sem, gate_sems, up_sems,
):
    me_x, core = place[0], place[1]
    count = cot.shape[0]
    n_z, _, wide, cols = gate_full.shape
    cot_copy = pltpu.make_async_copy(rows_ref.at[pl.ds(count, count)], cot, row_sem.at[0])
    down_copy = pltpu.make_async_copy(down_ref, down_full, down_sem.at[0])
    cot_copy.start()
    down_copy.start()
    gate_copies = copy_blocks((g0, g1, g2, g3), gate_full, gate_sems, me_x)
    up_copies = copy_blocks((u0, u1, u2, u3), up_full, up_sems, me_x)
    gate_value, up_value = gate_in[...], up_in[...]
    sigmoid_gate = sigmoid(gate_value)
    cot_copy.wait()
    down_copy.wait()
    hidden_grad = jnp.dot(
        cot[...], down_full[...].reshape(-1, cols), preferred_element_type=jnp.float32
    )
    gate_grad = (
        hidden_grad * up_value * sigmoid_gate * (1.0 + gate_value * (1.0 - sigmoid_gate))
    ).astype(jnp.bfloat16)
    up_grad = (hidden_grad * gate_value * sigmoid_gate).astype(jnp.bfloat16)
    grads = jnp.concatenate([gate_grad, up_grad], axis=1)
    for copy in gate_copies + up_copies:
        copy.wait()
    for out, which in ((other_out, 1 - core), (mine_out, core)):
        for y in range(0, n_z, 2):
            pair = [
                jnp.concatenate([gate_full[y + i, which], up_full[y + i, which]], axis=1)
                for i in range(2)
            ]
            value = dot(grads, jnp.concatenate(pair), ((1,), (1,))).astype(jnp.bfloat16)
            out[y] = value[:, :wide]
            out[y + 1] = value[:, wide:]


def call_kernel(kernel, n_smem_any, operands, out_shapes, scratch, flops):
    in_specs = [pl.BlockSpec(memory_space=pltpu.SMEM)]
    in_specs += [pl.BlockSpec(memory_space=pl.ANY)] * n_smem_any
    in_specs += [pl.BlockSpec(memory_space=pltpu.VMEM)] * (len(operands) - 1 - n_smem_any)
    return pl.pallas_call(
        kernel,
        out_shape=out_shapes,
        in_specs=in_specs,
        out_specs=[pl.BlockSpec(memory_space=pltpu.VMEM)] * len(out_shapes),
        scratch_shapes=scratch,
        compiler_params=pltpu.CompilerParams(vmem_limit_bytes=60 * 1024 * 1024),
        cost_estimate=pl.CostEstimate(flops=flops, bytes_accessed=10_000_000, transcendentals=0),
    )(*operands)


def sigmoid(value):
    return 1.0 / (1.0 + jnp.exp(-value))


def send_x(value, step):
    pairs = [
        (z * N_X + x, z * N_X + (x + step) % N_X) for z in range(N_Z) for x in range(N_X)
    ]
    return lax.ppermute(value, "fsdp", pairs)


def swap_z(value, flip):
    pairs = [(z * N_X + x, (z ^ flip) * N_X + x) for z in range(N_Z) for x in range(N_X)]
    return lax.ppermute(value, "fsdp", pairs)


def send_core(value):
    pairs = [(i, i ^ 1) for i in range(N_Y * N_CORE)]
    return lax.ppermute(value, "mp", pairs)


def copies_of(block):
    return jnp.broadcast_to(block[None], (N_Z,) + block.shape)


def gather_z(copies):
    return lax.all_to_all(copies, "fsdp", 0, 0, axis_index_groups=Z_GROUPS)


def add(left, right):
    return left.astype(jnp.float32) + right.astype(jnp.float32)


def on_device(tokens, cotangent, gate_weight, up_weight, down_weight):
    n_fsdp = lax.axis_size("fsdp")
    rows, width = tokens.shape
    depth, cols = gate_weight.shape
    n_feat = depth * n_fsdp
    factor = 1.0 / math.sqrt(rows * n_fsdp)
    me_x = lax.axis_index("fsdp") % N_X
    me_z = lax.axis_index("fsdp") // N_X
    core = lax.axis_index("mp") % N_CORE

    gate_copies = copies_of(gate_weight)
    gate_copies, tokens, cotangent = lax.optimization_barrier((gate_copies, tokens, cotangent))
    stacked = jnp.concatenate([tokens, cotangent])
    both = lax.all_gather(stacked, "mp", axis=1, tiled=True)

    down_x = jnp.zeros((N_X, depth, cols), down_weight.dtype)
    down_x = lax.dynamic_update_slice(down_x, down_weight[None], (me_x, 0, 0))
    for step in (1, N_X - 1, 2):
        block = send_x(down_weight, step)
        down_x = lax.dynamic_update_slice(down_x, block[None], ((me_x - step) % N_X, 0, 0))

    gate_z = gather_z(gate_copies)
    gate_left, gate_right = send_x(gate_z, 1), send_x(gate_z, -1)
    gate_z, up_copies = lax.optimization_barrier((gate_z, copies_of(up_weight)))
    up_z = gather_z(up_copies)
    up_z, down_copies, gate_left, gate_right = lax.optimization_barrier(
        (up_z, copies_of(down_x), gate_left, gate_right)
    )
    down_full = gather_z(down_copies).reshape(N_Z, N_CORE, 2 * depth, cols)

    up_right, up_left = send_x(up_z, -1), send_x(up_z, 1)
    gate_far, up_far = send_x(gate_left, 1), send_x(up_right, -1)
    blocks = (gate_z, gate_left, gate_right, gate_far, up_z, up_left, up_right, up_far)

    place = jnp.stack([me_x, core]).astype(jnp.int32)
    value = jax.ShapeDtypeStruct((rows, cols), jnp.float32)
    full = pltpu.VMEM((N_Z, N_CORE, 2 * depth, cols), jnp.bfloat16)
    row_block = pltpu.VMEM((rows, n_feat), jnp.bfloat16)
    sems = pltpu.SemaphoreType.DMA
    gate_value, up_value, down_partial = call_kernel(
        forward_kernel,
        9,
        (place, both) + blocks,
        (value, value, jax.ShapeDtypeStruct((2 * N_X, N_Z // 2, depth, cols), jnp.bfloat16)),
        [row_block, row_block, full, full, sems((2,)), sems((N_X,)), sems((N_X,))],
        6 * rows * n_feat * cols,
    )
    half = jax.ShapeDtypeStruct((N_Y, rows, width), jnp.bfloat16)
    other, mine = call_kernel(
        backward_kernel,
        10,
        (place, both, down_full) + blocks + (gate_value, up_value),
        (half, half),
        [row_block, full, full, full, sems((1,)), sems((1,)), sems((N_X,)), sems((N_X,))],
        6 * rows * n_feat * cols,
    )
    pair_sum = add(mine, send_core(other)).astype(jnp.bfloat16)
    summed = lax.all_to_all(pair_sum, "mp", 0, 0, axis_index_groups=Y_GROUPS)

    down_pair = lax.psum_scatter(
        down_partial.reshape(n_feat, cols),
        "fsdp",
        scatter_dimension=0,
        axis_index_groups=PAIR_GROUPS,
        tiled=True,
    ).reshape(N_Z // 2, depth, cols)
    block = lambda flip: lax.dynamic_index_in_dim(down_pair, (me_z // 2) ^ (flip // 2), 0, False)
    got = swap_z(jnp.stack([block(2), block(4)]), 2)
    got_last = swap_z(add(block(6), got[1]).astype(jnp.bfloat16), 6)
    down_sum = add(block(0), got[0]) + got_last.astype(jnp.float32)
    grad_down = (down_sum * factor).astype(jnp.bfloat16)
    input_grad = summed.astype(jnp.float32).sum(0).astype(jnp.bfloat16)
    return (input_grad, grad_down)


def solution(mesh):
    placed = P("fsdp", "mp")
    return jax.shard_map(
        on_device,
        mesh=mesh,
        in_specs=(placed,) * 5,
        out_specs=(placed, placed),
        check_vma=False,
    )
```

```python
import math

import jax
import jax.numpy as jnp
from jax import lax
from jax.experimental import pallas as pl
from jax.experimental.pallas import tpu as pltpu
from jax.sharding import PartitionSpec as P

N_Z = 8
N_X = 4
N_Y = 8
N_CORE = 2
Z_GROUPS = [[z * N_X + x for z in range(N_Z)] for x in range(N_X)]
PAIR_GROUPS = [
    [z * N_X + x for x in range(N_X)] + [(z + 1) * N_X + x for x in reversed(range(N_X))]
    for z in range(0, N_Z, 2)
]
Y_GROUPS = [[y * N_CORE + c for y in range(N_Y)] for c in range(N_CORE)]


def dot(left, right, dims):
    return lax.dot_general(left, right, (dims, ((), ())), preferred_element_type=jnp.float32)


def pair_place(odd, x):
    return 2 * N_X - 1 - x if odd else x


def copy_blocks(blocks, full, sems, me_x):
    depth = blocks[0].shape[1]
    copies = []
    for i, step in enumerate((0, N_X - 1, 1, 2)):
        x = lax.rem(me_x + step, N_X)
        row = pl.multiple_of(lax.rem(x, 2) * depth, depth)
        target = full.at[:, lax.div(x, 2), pl.ds(row, depth), :]
        copies.append(pltpu.make_async_copy(blocks[i], target, sems.at[i]))
    for copy in copies:
        copy.start()
    return copies


def forward_kernel(
    place, rows_ref, g0, g1, g2, g3, u0, u1, u2, u3, gate_out, up_out, partial_out,
    tok, cot, gate_full, up_full, row_sems, gate_sems, up_sems,
):
    count, n_feat = tok.shape
    tok_copy = pltpu.make_async_copy(rows_ref.at[pl.ds(0, count)], tok, row_sems.at[0])
    cot_copy = pltpu.make_async_copy(rows_ref.at[pl.ds(count, count)], cot, row_sems.at[1])
    tok_copy.start()
    gate_copies = copy_blocks((g0, g1, g2, g3), gate_full, gate_sems, place[0])
    up_copies = copy_blocks((u0, u1, u2, u3), up_full, up_sems, place[0])
    cot_copy.start()
    tok_copy.wait()
    for copy in gate_copies:
        copy.wait()
    gate_value = jnp.dot(
        tok[...], gate_full[...].reshape(n_feat, -1), preferred_element_type=jnp.float32
    )
    gate_out[...] = gate_value
    for copy in up_copies:
        copy.wait()
    up_value = jnp.dot(
        tok[...], up_full[...].reshape(n_feat, -1), preferred_element_type=jnp.float32
    )
    up_out[...] = up_value
    hidden = (gate_value * sigmoid(gate_value) * up_value).astype(jnp.bfloat16)
    cot_copy.wait()
    partial_value = dot(cot[...], hidden, ((0,), (0,))).astype(jnp.bfloat16)
    depth = n_feat // (N_Z * N_X)
    for z in range(N_Z):
        for x in range(N_X):
            row = (z * N_X + x) * depth
            partial_out[pair_place(z % 2, x), z // 2] = partial_value[row : row + depth]


def backward_kernel(
    place, rows_ref, down_ref, g0, g1, g2, g3, u0, u1, u2, u3, gate_in, up_in, other_out, mine_out,
    cot, down_full, gate_full, up_full, row_sem, down_sem, gate_sems, up_sems,
):
    me_x, core = place[0], place[1]
    count = cot.shape[0]
    n_z, _, wide, cols = gate_full.shape
    cot_copy = pltpu.make_async_copy(rows_ref.at[pl.ds(count, count)], cot, row_sem.at[0])
    down_copy = pltpu.make_async_copy(down_ref, down_full, down_sem.at[0])
    cot_copy.start()
    down_copy.start()
    gate_copies = copy_blocks((g0, g1, g2, g3), gate_full, gate_sems, me_x)
    up_copies = copy_blocks((u0, u1, u2, u3), up_full, up_sems, me_x)
    gate_value, up_value = gate_in[...], up_in[...]
    sigmoid_gate = sigmoid(gate_value)
    cot_copy.wait()
    down_copy.wait()
    hidden_grad = jnp.dot(
        cot[...], down_full[...].reshape(-1, cols), preferred_element_type=jnp.float32
    )
    gate_grad = (
        hidden_grad * up_value * sigmoid_gate * (1.0 + gate_value * (1.0 - sigmoid_gate))
    ).astype(jnp.bfloat16)
    up_grad = (hidden_grad * gate_value * sigmoid_gate).astype(jnp.bfloat16)
    grads = jnp.concatenate([gate_grad, up_grad], axis=1)
    for copy in gate_copies + up_copies:
        copy.wait()
    for out, which in ((other_out, 1 - core), (mine_out, core)):
        for y in range(0, n_z, 2):
            pair = [
                jnp.concatenate([gate_full[y + i, which], up_full[y + i, which]], axis=1)
                for i in range(2)
            ]
            value = dot(grads, jnp.concatenate(pair), ((1,), (1,))).astype(jnp.bfloat16)
            out[y] = value[:, :wide]
            out[y + 1] = value[:, wide:]


def call_kernel(kernel, n_smem_any, operands, out_shapes, scratch, flops):
    in_specs = [pl.BlockSpec(memory_space=pltpu.SMEM)]
    in_specs += [pl.BlockSpec(memory_space=pl.ANY)] * n_smem_any
    in_specs += [pl.BlockSpec(memory_space=pltpu.VMEM)] * (len(operands) - 1 - n_smem_any)
    return pl.pallas_call(
        kernel,
        out_shape=out_shapes,
        in_specs=in_specs,
        out_specs=[pl.BlockSpec(memory_space=pltpu.VMEM)] * len(out_shapes),
        scratch_shapes=scratch,
        compiler_params=pltpu.CompilerParams(vmem_limit_bytes=60 * 1024 * 1024),
        cost_estimate=pl.CostEstimate(flops=flops, bytes_accessed=10_000_000, transcendentals=0),
    )(*operands)


def sigmoid(value):
    return 1.0 / (1.0 + jnp.exp(-value))


def send_x(value, step):
    pairs = [
        (z * N_X + x, z * N_X + (x + step) % N_X) for z in range(N_Z) for x in range(N_X)
    ]
    return lax.ppermute(value, "fsdp", pairs)


def swap_z(value, flip):
    pairs = [(z * N_X + x, (z ^ flip) * N_X + x) for z in range(N_Z) for x in range(N_X)]
    return lax.ppermute(value, "fsdp", pairs)


def send_core(value):
    pairs = [(i, i ^ 1) for i in range(N_Y * N_CORE)]
    return lax.ppermute(value, "mp", pairs)


def copies_of(block):
    return jnp.broadcast_to(block[None], (N_Z,) + block.shape)


def gather_z(copies):
    return lax.all_to_all(copies, "fsdp", 0, 0, axis_index_groups=Z_GROUPS)


def add(left, right):
    return left.astype(jnp.float32) + right.astype(jnp.float32)


def on_device(tokens, cotangent, gate_weight, up_weight, down_weight):
    n_fsdp = lax.axis_size("fsdp")
    rows, width = tokens.shape
    depth, cols = gate_weight.shape
    n_feat = depth * n_fsdp
    factor = 1.0 / math.sqrt(rows * n_fsdp)
    me_x = lax.axis_index("fsdp") % N_X
    me_z = lax.axis_index("fsdp") // N_X
    core = lax.axis_index("mp") % N_CORE

    gate_copies = copies_of(gate_weight)
    gate_copies, tokens, cotangent = lax.optimization_barrier((gate_copies, tokens, cotangent))
    stacked = jnp.concatenate([tokens, cotangent])
    both = lax.all_gather(stacked, "mp", axis=1, tiled=True)

    down_x = jnp.zeros((N_X, depth, cols), down_weight.dtype)
    down_x = lax.dynamic_update_slice(down_x, down_weight[None], (me_x, 0, 0))
    for step in (1, N_X - 1, 2):
        block = send_x(down_weight, step)
        down_x = lax.dynamic_update_slice(down_x, block[None], ((me_x - step) % N_X, 0, 0))

    gate_z = gather_z(gate_copies)
    gate_left, gate_right = send_x(gate_z, 1), send_x(gate_z, -1)
    gate_z, up_copies = lax.optimization_barrier((gate_z, copies_of(up_weight)))
    up_z = gather_z(up_copies)
    up_z, down_copies, gate_left, gate_right = lax.optimization_barrier(
        (up_z, copies_of(down_x), gate_left, gate_right)
    )
    down_full = gather_z(down_copies).reshape(N_Z, N_CORE, 2 * depth, cols)

    up_right, up_left = send_x(up_z, -1), send_x(up_z, 1)
    gate_far, up_far = send_x(gate_left, 1), send_x(up_right, -1)
    blocks = (gate_z, gate_left, gate_right, gate_far, up_z, up_left, up_right, up_far)

    place = jnp.stack([me_x, core]).astype(jnp.int32)
    value = jax.ShapeDtypeStruct((rows, cols), jnp.float32)
    full = pltpu.VMEM((N_Z, N_CORE, 2 * depth, cols), jnp.bfloat16)
    row_block = pltpu.VMEM((rows, n_feat), jnp.bfloat16)
    sems = pltpu.SemaphoreType.DMA
    gate_value, up_value, down_partial = call_kernel(
        forward_kernel,
        9,
        (place, both) + blocks,
        (value, value, jax.ShapeDtypeStruct((2 * N_X, N_Z // 2, depth, cols), jnp.bfloat16)),
        [row_block, row_block, full, full, sems((2,)), sems((N_X,)), sems((N_X,))],
        6 * rows * n_feat * cols,
    )
    half = jax.ShapeDtypeStruct((N_Y, rows, width), jnp.bfloat16)
    other, mine = call_kernel(
        backward_kernel,
        10,
        (place, both, down_full) + blocks + (gate_value, up_value),
        (half, half),
        [row_block, full, full, full, sems((1,)), sems((1,)), sems((N_X,)), sems((N_X,))],
        6 * rows * n_feat * cols,
    )
    pair_sum = add(mine, send_core(other)).astype(jnp.bfloat16)
    summed = lax.all_to_all(pair_sum, "mp", 0, 0, axis_index_groups=Y_GROUPS)

    down_pair = lax.psum_scatter(
        down_partial.reshape(n_feat, cols),
        "fsdp",
        scatter_dimension=0,
        axis_index_groups=PAIR_GROUPS,
        tiled=True,
    ).reshape(N_Z // 2, depth, cols)
    block = lambda flip: lax.dynamic_index_in_dim(down_pair, (me_z // 2) ^ (flip // 2), 0, False)
    got = swap_z(jnp.stack([block(2), block(4)]), 2)
    kept, passed = lax.optimization_barrier(
        (add(block(0), got[0]), add(block(6), got[1]).astype(jnp.bfloat16))
    )
    down_sum = kept + swap_z(passed, 6).astype(jnp.float32)
    grad_down = (down_sum * factor).astype(jnp.bfloat16)
    input_grad = summed.astype(jnp.float32).sum(0).astype(jnp.bfloat16)
    return (input_grad, grad_down)


def solution(mesh):
    placed = P("fsdp", "mp")
    return jax.shard_map(
        on_device,
        mesh=mesh,
        in_specs=(placed,) * 5,
        out_specs=(placed, placed),
        check_vma=False,
    )
```
